256 devices in a mesh: proto: 64 (over x, z, core), crop: 4 (over y).
Axes of the slice: x: 4, y: 4, z: 8, core: 2. Of those that a mesh axis runs over, the one named last changes fastest.
Arguments:
- teacher_feats: float32 [384, 2048], P('proto', 'crop'), may hold values from -4 to 4
- student_feats: float32 [384, 2048], P('proto', 'crop'), may hold values from -4 to 4
- prototypes: float32 [384, 131072], P(None, 'proto'), may hold values from -4 to 4
Outputs:
- grad_features: float32 [384, 2048], P('proto', 'crop')
- grad_protos: float32 [384, 131072], P('crop', 'proto')
- loss: float32 [], replicated
The draws below stay inside these ranges and needn't reach their ends.
All inputs are finite; a program needn't handle non-finite values.
Results may differ from the reference program's by a relative error of at most 0.0003.
Values sent between devices are 32-bit elements; how exact they have to be, the bound alone decides.
A program may use at most 64 MiB of HBM per device.

```python
import math
import jax
import jax.numpy as jnp
import numpy as np
from jax import lax

D = 384
K = 131072
CROPS = 2048
ITERS = 3


cluster_count = 16


cluster_bounds = np.cumsum(np.arange(1, cluster_count + 1))[:-1]


weight_total = 136


value_bound = 4.0


def centers_of(key):
    return jax.random.normal(jax.random.fold_in(key, 100), (D, cluster_count), jnp.float32)


def crop_groups(key):
    ticket = jax.random.randint(jax.random.fold_in(key, 101), (CROPS,), 0, weight_total)
    bounds = jnp.asarray(cluster_bounds, jnp.int32)
    position = jnp.sum((ticket[None, :] >= bounds[:, None]).astype(jnp.int32), axis=0)
    shuffle = jax.random.permutation(jax.random.fold_in(key, 102), cluster_count)
    return jnp.take(shuffle, position)


def crop_shared(key):
    centers = centers_of(key)
    groups = crop_groups(key)
    image_noise = jax.random.normal(jax.random.fold_in(key, 103), (D, CROPS), jnp.float32)
    return jnp.take(centers, groups, axis=1) + 0.8 * image_noise


def column_scales(key, lower, upper, count):
    return jnp.exp(jax.random.uniform(key, (1, count), jnp.float32, math.log(lower), math.log(upper)))


def draw_teacher_feats(key, part):
    shared = crop_shared(key)
    key = jax.random.fold_in(key, 1)
    noise_key, scale_key = jax.random.split(key)
    view_noise = jax.random.normal(noise_key, (D, CROPS), jnp.float32)
    scales = column_scales(scale_key, 0.1, 1.0, CROPS)
    return jnp.clip((shared + 0.5 * view_noise) * scales, -value_bound, value_bound)


def draw_student_feats(key, part):
    shared = crop_shared(key)
    key = jax.random.fold_in(key, 2)
    noise_key, scale_key = jax.random.split(key)
    view_noise = jax.random.normal(noise_key, (D, CROPS), jnp.float32)
    scales = column_scales(scale_key, 0.1, 1.0, CROPS)
    return jnp.clip((shared + 0.5 * view_noise) * scales, -value_bound, value_bound)


def draw_prototypes(key, part):
    centers = centers_of(key)
    key = jax.random.fold_in(key, 3)
    group_key, noise_key, scale_key = jax.random.split(key, 3)
    groups = jax.random.randint(group_key, (K,), 0, cluster_count)
    own_noise = jax.random.normal(noise_key, (D, K), jnp.float32)
    scales = column_scales(scale_key, 0.1, 1.0, K)
    return jnp.clip((jnp.take(centers, groups, axis=1) + own_noise) * scales, -value_bound, value_bound)


def setup_inputs(seed: int = 0) -> dict:
    key_of = jax.random.split(jax.random.key(seed), 4)
    return {
        "teacher_feats": draw_teacher_feats(jax.random.fold_in(key_of[3], 71), 0),
        "student_feats": draw_student_feats(jax.random.fold_in(key_of[3], 71), 0),
        "prototypes": draw_prototypes(jax.random.fold_in(key_of[3], 71), 0),
    }


teacher_temp = 0.07
student_temp = 0.1
norm_eps = 1e-06
highest = lax.Precision.HIGHEST

def unit_columns(matrix):
    return matrix / jnp.sqrt(lax.optimization_barrier(jnp.sum(matrix * matrix, axis=0, keepdims=True)) + norm_eps)

def reference(teacher_feats, student_feats, prototypes):
    crops = teacher_feats.shape[1]
    protos = prototypes.shape[1]
    width = prototypes.shape[0]
    weights = unit_columns(prototypes)
    teacher = unit_columns(teacher_feats)
    student = unit_columns(student_feats)
    block = min(128, crops)
    blocks = crops // block
    teacher_rows = teacher.T.reshape(blocks, block, width)
    student_rows = student.T.reshape(blocks, block, width)
    scale = math.sqrt(protos)

    def expo(rows):
        return jnp.exp(jnp.dot(rows, weights, precision=highest, preferred_element_type=jnp.float32) / teacher_temp)

    def first_pass(carry, rows):
        return (carry + lax.optimization_barrier(jnp.sum(expo(rows), axis=0)), None)
    totals, _ = lax.scan(first_pass, jnp.zeros((protos,), jnp.float32), teacher_rows)
    scaling = 1.0 / totals
    for step in range(ITERS - 1):

        def middle_pass(carry, rows):
            values = expo(rows)
            crop_scale = 1.0 / lax.optimization_barrier(jnp.sum(values * scaling[None, :], axis=1))
            return (carry + lax.optimization_barrier(jnp.sum(values * crop_scale[:, None], axis=0)), None)
        totals, _ = lax.scan(middle_pass, jnp.zeros((protos,), jnp.float32), teacher_rows)
        scaling = 1.0 / totals

    def final_pass(carry, pair):
        grad_sum, loss_sum = carry
        trows, srows = pair
        values = expo(trows)
        crop_scale = 1.0 / lax.optimization_barrier(jnp.sum(values * scaling[None, :], axis=1))
        targets = values * scaling[None, :] * crop_scale[:, None]
        logits = jnp.dot(srows, weights, precision=highest, preferred_element_type=jnp.float32) / student_temp
        lse = jnp.log(lax.optimization_barrier(jnp.sum(jnp.exp(logits), axis=1)))
        probs = jnp.exp(logits - lse[:, None])
        loss_sum = loss_sum + jnp.sum(lse) - jnp.sum(targets * logits)
        grads = (probs - targets) * (scale / student_temp)
        feat_block = jnp.dot(grads, weights.T, precision=highest, preferred_element_type=jnp.float32)
        grad_sum = grad_sum + jnp.dot(srows.T, grads, precision=highest, preferred_element_type=jnp.float32)
        return ((grad_sum, loss_sum), feat_block)
    init = (jnp.zeros((width, protos), jnp.float32), jnp.zeros((), jnp.float32))
    (grad_protos, loss_sum), feat_blocks = lax.scan(final_pass, init, (teacher_rows, student_rows))
    grad_features = feat_blocks.reshape(crops, width).T
    return (grad_features, grad_protos, loss_sum / crops)
```

```python
import functools
import math

import jax
import jax.numpy as jnp
from jax import lax
from jax.experimental import pallas as pl
from jax.experimental.pallas import tpu as pltpu
from jax.sharding import PartitionSpec as P

MESH = pl.DeviceIdType.MESH
TEACHER_TEMP = 0.07
STUDENT_TEMP = 0.1
EPS = 1e-06
ITERS = 3
f32 = jnp.float32
bf16 = jnp.bfloat16
LANES = 128


def split(x):
    hi = x.astype(bf16)
    return hi, (x - hi.astype(f32)).astype(bf16)


def await_bytes(ref, sem):
    pltpu.make_async_copy(ref, ref, sem).wait()


def nn(a, b):
    return lax.dot_general(a, b, (((1,), (0,)), ((), ())), preferred_element_type=f32)


def nt(a, b):
    return lax.dot_general(a, b, (((1,), (1,)), ((), ())), preferred_element_type=f32)


def kernel(
    n_y, n_chip, scale, crops_all,
    t_ref, s_ref, w_ref,
    gf_ref, gp_ref, loss_ref,
    gt, gs, flat, zt_cat, zs_cat, zs_hi, zs_lo, w_cat, e_ref, s_log, es_ref, g_hi, g_lo,
    tcol, vcol, col_out, col_in, ubuf, row_out, row_in, gf_acc, rs_flat, rs_src, rs_pair, rs_in,
    loss_in,
    sem_g_s, sem_g_r, sem_d_s, sem_d_r, sem_c_s, sem_c_r, sem_r_s, sem_r_r, sem_f_s, sem_f_r,
    sem_l_s, sem_l_r,
):
    p = lax.axis_index("proto")
    y = lax.axis_index("crop")
    chip = p // 2
    core = p % 2
    width, protos = w_ref.shape
    crops = e_ref.shape[0]
    n_ct = crops // LANES
    n_pt = protos // LANES
    feat = width // (2 * n_chip)
    n_plane = 2 * n_chip

    bar = pltpu.get_barrier_semaphore()

    def greet_plane(i, c):
        pl.semaphore_signal(bar, inc=1, device_id=(lax.rem(p + i, n_plane), y), device_id_type=MESH)
        return c

    lax.fori_loop(1, n_plane, greet_plane, 0)
    for i in range(1, n_y):
        pl.semaphore_signal(bar, inc=1, device_id=(p, lax.rem(y + i, n_y)), device_id_type=MESH)

    for src, dst in ((t_ref, gt), (s_ref, gs)):
        for j in range(feat):
            for ct in range(n_ct):
                k = n_ct * j + ct
                dst[chip, core, k : k + 1, :] = src[j : j + 1, ct * LANES : (ct + 1) * LANES]

    def prep_w(i, c):
        cols = pl.ds(pl.multiple_of(i * 256, 256), 256)
        w = w_ref[:, cols]
        w = w * (1.0 / jnp.sqrt(jnp.sum(w * w, axis=0, keepdims=True) + EPS))
        hi, lo = split(w)
        w_cat[0:width, cols] = hi
        w_cat[width : 2 * width, cols] = hi
        w_cat[2 * width : 3 * width, cols] = lo
        return c

    lax.fori_loop(0, protos // 256, prep_w, 0)
    pl.semaphore_wait(bar, n_plane - 1 + n_y - 1)

    def gather_start(buf, k):
        def go(i, c):
            other = lax.rem(chip + i, n_chip)
            pltpu.make_async_remote_copy(
                src_ref=buf.at[chip, core],
                dst_ref=buf.at[chip, core],
                send_sem=sem_g_s.at[k],
                recv_sem=sem_g_r.at[k],
                device_id=(other * 2 + core, y),
                device_id_type=MESH,
            ).start()
            return c

        lax.fori_loop(1, n_chip, go, 0)

    def gather_finish(buf, k):
        await_bytes(buf.at[pl.ds(0, n_chip - 1), core], sem_g_r.at[k])
        await_bytes(buf.at[pl.ds(0, n_chip - 1), core], sem_g_s.at[k])
        cp = pltpu.make_async_remote_copy(
            src_ref=buf.at[:, core],
            dst_ref=buf.at[:, core],
            send_sem=sem_d_s.at[k],
            recv_sem=sem_d_r.at[k],
            device_id=(p + 1 - 2 * core, y),
            device_id_type=MESH,
        )
        cp.start()
        return cp

    def unit(buf, temp, cat, keep):
        flat[...] = buf[...].reshape(flat.shape)
        for ct in range(n_ct):
            rows = pl.ds(ct * LANES, LANES)
            x = flat[pl.ds(ct, width, stride=n_ct), :]
            x = x * (1.0 / jnp.sqrt(jnp.sum(x * x, axis=0, keepdims=True) + EPS))
            if keep:
                hi, lo = split(x)
                zs_hi[:, rows] = hi
                zs_lo[:, rows] = lo
            xt = (x * (1.0 / temp)).T
            hi, lo = split(xt)
            cat[rows, 0:width] = hi
            cat[rows, width : 2 * width] = lo
            cat[rows, 2 * width : 3 * width] = hi

    def col_start(k):
        col_in[k, pl.ds(y, 1)] = col_out[k : k + 1]
        for i in range(1, n_y):
            pltpu.make_async_remote_copy(
                src_ref=col_out.at[k],
                dst_ref=col_in.at[k, y],
                send_sem=sem_c_s.at[k],
                recv_sem=sem_c_r.at[k],
                device_id=(p, lax.rem(y + i, n_y)),
                device_id_type=MESH,
            ).start()

    def col_finish(k):
        await_bytes(col_in.at[k, pl.ds(0, n_y - 1)], sem_c_r.at[k])
        total = col_in[k, 0]
        for i in range(1, n_y):
            total = total + col_in[k, i]
        ubuf[...] = 1.0 / total

    def row_start(k):
        row_in[k, pl.ds(p, 1)] = row_out[k : k + 1]

        def go(i, c):
            pltpu.make_async_remote_copy(
                src_ref=row_out.at[k],
                dst_ref=row_in.at[k, p],
                send_sem=sem_r_s.at[k],
                recv_sem=sem_r_r.at[k],
                device_id=(lax.rem(p + i, n_plane), y),
                device_id_type=MESH,
            ).start()
            return c

        lax.fori_loop(1, n_plane, go, 0)

    def row_finish(k):
        await_bytes(row_in.at[k, pl.ds(0, n_plane - 1)], sem_r_r.at[k])
        return jnp.sum(row_in[k], axis=0)

    def to_rows(k):
        for ct in range(n_ct):
            block = tcol[ct * LANES : (ct + 1) * LANES, :].T
            row_out[k, ct : ct + 1, :] = jnp.sum(block, axis=0, keepdims=True)

    def to_column(values):
        for ct in range(n_ct):
            row = jnp.broadcast_to(values[ct : ct + 1, :], (LANES, LANES))
            vcol[ct * LANES : (ct + 1) * LANES, :] = row.T

    chunk = 64

    def lane_fold(x):
        total = x[:, 0:LANES]
        for j in range(1, n_pt):
            total = total + x[:, j * LANES : (j + 1) * LANES]
        return total

    def scaled_fold(rows, mult):
        total = None
        for j in range(n_pt):
            x = e_ref[rows, j * LANES : (j + 1) * LANES]
            if mult is not None:
                x = x * mult[rows, j * LANES : (j + 1) * LANES]
            x = x * ubuf[j : j + 1, :]
            total = x if total is None else total + x
        return total

    def row_pass(k, mult):
        def go(i, c):
            rows = pl.ds(pl.multiple_of(i * chunk, chunk), chunk)
            tcol[rows, :] = scaled_fold(rows, mult)
            return c

        lax.fori_loop(0, crops // chunk, go, 0)
        to_rows(k)

    def col_pass(k):
        def go(i, acc):
            rows = pl.ds(pl.multiple_of(i * 32, 32), 32)
            v = vcol[rows, :]
            out = []
            for j in range(n_pt):
                x = e_ref[rows, j * LANES : (j + 1) * LANES] * v
                out.append(acc[j] + jnp.sum(x.reshape(4, 8, LANES), axis=0))
            return tuple(out)

        acc = lax.fori_loop(0, crops // 32, go, tuple(jnp.zeros((8, LANES), f32) for _ in range(n_pt)))
        for j in range(n_pt):
            col_out[k, j : j + 1, :] = jnp.sum(acc[j], axis=0, keepdims=True)

    gather_start(gt, 0)
    pair_t = gather_finish(gt, 0)
    gather_start(gs, 1)
    pair_t.wait()
    unit(gt, TEACHER_TEMP, zt_cat, False)

    def teacher_block(i, c):
        cols = pl.ds(pl.multiple_of(i * 256, 256), 256)
        e = jnp.exp(nn(zt_cat[...], w_cat[:, cols]))
        e_ref[:, cols] = e
        sums = jnp.sum(e, axis=0, keepdims=True)
        col_out[0, pl.ds(2 * i, 1), :] = sums[:, 0:LANES]
        col_out[0, pl.ds(2 * i + 1, 1), :] = sums[:, LANES : 2 * LANES]
        return c

    lax.fori_loop(0, protos // 256, teacher_block, 0)
    col_start(0)
    pair_s = gather_finish(gs, 1)
    col_finish(0)
    row_pass(0, None)
    row_start(0)

    pair_s.wait()
    unit(gs, STUDENT_TEMP, zs_cat, True)

    def student_block(i, c):
        cols = pl.ds(pl.multiple_of(i * 256, 256), 256)
        s = nn(zs_cat[...], w_cat[:, cols])
        s_log[:, cols] = s
        es_ref[:, cols] = jnp.exp(s)
        return c

    lax.fori_loop(0, protos // 256, student_block, 0)
    for k in (1, 2):
        to_column(1.0 / row_finish(k - 1))
        col_pass(k)
        col_start(k)
        if k == 1:
            def fold(i, c):
                rows = pl.ds(pl.multiple_of(i * chunk, chunk), chunk)
                tcol[rows, :] = lane_fold(es_ref[rows, :])
                return c

            lax.fori_loop(0, crops // chunk, fold, 0)
            to_rows(3)
            row_start(3)
        col_finish(k)
        row_pass(k, None)
        row_start(k)
    row_pass(4, s_log)
    row_start(4)
    last = row_finish(2)
    student_total = row_finish(3)
    cross = row_finish(4)
    to_column(scale / last)
    tv = scale / student_total
    for ct in range(n_ct):
        row = jnp.broadcast_to(tv[ct : ct + 1, :], (LANES, LANES))
        tcol[ct * LANES : (ct + 1) * LANES, :] = row.T
    loss_in[pl.ds(y, 1)] = (jnp.log(student_total) - cross / last)[None]
    for i in range(1, n_y):
        pltpu.make_async_remote_copy(
            src_ref=loss_in.at[y],
            dst_ref=loss_in.at[y],
            send_sem=sem_l_s.at[0],
            recv_sem=sem_l_r.at[0],
            device_id=(p, lax.rem(y + i, n_y)),
            device_id_type=MESH,
        ).start()

    def grad_block(i, c):
        rows = pl.ds(pl.multiple_of(i * 32, 32), 32)
        v = vcol[rows, :]
        t = tcol[rows, :]
        for j in range(n_pt):
            lanes = slice(j * LANES, (j + 1) * LANES)
            g = es_ref[rows, lanes] * t - e_ref[rows, lanes] * ubuf[j : j + 1, :] * v
            hi, lo = split(g)
            g_hi[rows, lanes] = hi
            g_lo[rows, lanes] = lo
        return c

    lax.fori_loop(0, crops // 32, grad_block, 0)

    gf_acc[...] = jnp.zeros_like(gf_acc)

    def feat_block(i, c):
        cols = pl.ds(pl.multiple_of(i * 512, 512), 512)
        w_hi = w_cat[0:width, cols]
        w_lo = w_cat[2 * width : 3 * width, cols]
        gf_acc[...] += nt(w_hi, g_hi[:, cols]) + nt(w_hi, g_lo[:, cols]) + nt(w_lo, g_hi[:, cols])
        return c

    lax.fori_loop(0, protos // 512, feat_block, 0)
    for ct in range(n_ct):
        rs_flat[pl.ds(ct, width, stride=n_ct), :] = gf_acc[:, ct * LANES : (ct + 1) * LANES]
    rs_src[...] = rs_flat[...].reshape(rs_src.shape)
    pair = pltpu.make_async_remote_copy(
        src_ref=rs_src.at[:, 1 - core],
        dst_ref=rs_pair,
        send_sem=sem_f_s.at[0],
        recv_sem=sem_f_r.at[0],
        device_id=(p + 1 - 2 * core, y),
        device_id_type=MESH,
    )
    pair.start()
    pair.wait()
    rs_pair[...] += rs_src[:, core]
    rs_in[pl.ds(chip, 1)] = rs_pair[pl.ds(chip, 1)]

    def scatter(i, c):
        other = lax.rem(chip + i, n_chip)
        pltpu.make_async_remote_copy(
            src_ref=rs_pair.at[other],
            dst_ref=rs_in.at[chip],
            send_sem=sem_f_s.at[1],
            recv_sem=sem_f_r.at[1],
            device_id=(other * 2 + core, y),
            device_id_type=MESH,
        ).start()
        return c

    lax.fori_loop(1, n_chip, scatter, 0)

    def proto_block(i, c):
        cols = pl.ds(pl.multiple_of(i * 256, 256), 256)
        a = g_hi[:, cols]
        gp_ref[:, cols] = nn(zs_hi[...], a) + nn(zs_lo[...], a) + nn(zs_hi[...], g_lo[:, cols])
        return c

    lax.fori_loop(0, protos // 256, proto_block, 0)

    await_bytes(loss_in.at[pl.ds(0, n_y - 1)], sem_l_r.at[0])
    loss_ref[0, 0] = jnp.sum(jnp.sum(loss_in[...], axis=0)) * (1.0 / crops_all)
    await_bytes(rs_in.at[pl.ds(0, n_chip - 1)], sem_f_r.at[1])
    total = jnp.sum(rs_in[...], axis=0)
    for j in range(feat):
        for ct in range(n_ct):
            k = n_ct * j + ct
            gf_ref[j : j + 1, ct * LANES : (ct + 1) * LANES] = total[k : k + 1, :]

    pair_t_sem = None
    await_bytes(loss_in.at[pl.ds(0, n_y - 1)], sem_l_s.at[0])
    await_bytes(rs_in.at[pl.ds(0, n_chip - 1)], sem_f_s.at[1])
    for k in range(3):
        await_bytes(col_in.at[k, pl.ds(0, n_y - 1)], sem_c_s.at[k])
    for k in range(5):
        await_bytes(row_in.at[k, pl.ds(0, n_plane - 1)], sem_r_s.at[k])


def on_device(n_y, n_chip, t, s, w):
    width, protos = w.shape
    feat, crops = t.shape
    n_ct = crops // LANES
    n_pt = protos // LANES
    n_plane = 2 * n_chip
    scale = math.sqrt(protos * n_plane) / STUDENT_TEMP
    vm = pltpu.VMEM
    dma = pltpu.SemaphoreType.DMA
    slots = (n_chip, 2, feat * n_ct, LANES)
    gf, gp, loss = pl.pallas_call(
        functools.partial(kernel, n_y, n_chip, scale, crops * n_y),
        out_shape=(
            jax.ShapeDtypeStruct((feat, crops), f32),
            jax.ShapeDtypeStruct((width, protos), f32),
            jax.ShapeDtypeStruct((1, 1), f32),
        ),
        in_specs=[pl.BlockSpec(memory_space=vm)] * 3,
        out_specs=(
            pl.BlockSpec(memory_space=vm),
            pl.BlockSpec(memory_space=vm),
            pl.BlockSpec(memory_space=pltpu.SMEM),
        ),
        scratch_shapes=[
            vm(slots, f32),
            vm(slots, f32),
            vm((width * n_ct, LANES), f32),
            vm((crops, 3 * width), bf16),
            vm((crops, 3 * width), bf16),
            vm((width, crops), bf16),
            vm((width, crops), bf16),
            vm((3 * width, protos), bf16),
            vm((crops, protos), f32),
            vm((crops, protos), f32),
            vm((crops, protos), f32),
            vm((crops, protos), bf16),
            vm((crops, protos), bf16),
            vm((crops, LANES), f32),
            vm((crops, LANES), f32),
            vm((3, n_pt, LANES), f32),
            vm((3, n_y, n_pt, LANES), f32),
            vm((n_pt, LANES), f32),
            vm((5, n_ct, LANES), f32),
            vm((5, n_plane, n_ct, LANES), f32),
            vm((width, crops), f32),
            vm((width * n_ct, LANES), f32),
            vm(slots, f32),
            vm((n_chip, feat * n_ct, LANES), f32),
            vm((n_chip, feat * n_ct, LANES), f32),
            vm((n_y, n_ct, LANES), f32),
            dma((2,)), dma((2,)), dma((2,)), dma((2,)), dma((3,)), dma((3,)), dma((5,)), dma((5,)),
            dma((2,)), dma((2,)), dma((1,)), dma((1,)),
        ],
        compiler_params=pltpu.CompilerParams(
            collective_id=0, has_side_effects=True, vmem_limit_bytes=60 * 2**20
        ),
    )(t, s, w)
    gp = lax.psum_scatter(gp, "crop", scatter_dimension=0, tiled=True)
    return gf, gp, loss.reshape(())


def solution(mesh):
    placed = (P("proto", "crop"), P("proto", "crop"), P(None, "proto"))
    n_y = mesh.shape["crop"]
    n_chip = mesh.shape["proto"] // 2
    return jax.shard_map(
        functools.partial(on_device, n_y, n_chip),
        mesh=mesh,
        in_specs=placed,
        out_specs=(P("proto", "crop"), P("crop", "proto"), P()),
        check_vma=False,
    )
```

```python
import functools
import math

import jax
import jax.numpy as jnp
from jax import lax
from jax.experimental import pallas as pl
from jax.experimental.pallas import tpu as pltpu
from jax.sharding import PartitionSpec as P

MESH = pl.DeviceIdType.MESH
TEACHER_TEMP = 0.07
STUDENT_TEMP = 0.1
EPS = 1e-06
ITERS = 3
f32 = jnp.float32
bf16 = jnp.bfloat16
LANES = 128


def split(x):
    hi = x.astype(bf16)
    return hi, (x - hi.astype(f32)).astype(bf16)


def await_bytes(ref, sem):
    pltpu.make_async_copy(ref, ref, sem).wait()


def nn(a, b):
    return lax.dot_general(a, b, (((1,), (0,)), ((), ())), preferred_element_type=f32)


def nt(a, b):
    return lax.dot_general(a, b, (((1,), (1,)), ((), ())), preferred_element_type=f32)


def kernel(
    n_y, n_chip, scale, crops_all,
    t_ref, s_ref, w_ref,
    gf_ref, gp_ref, loss_ref,
    gt, gs, flat, zt_cat, zs_cat, zs_hi, zs_lo, w_cat, e_ref, s_log, es_ref, g_hi, g_lo,
    tcol, vcol, col_out, col_in, ubuf, row_out, row_in, gf_acc, rs_flat, rs_src, rs_pair, rs_in,
    loss_in, w_raw, part, relay, final,
    sem_g_s, sem_g_r, sem_d_s, sem_d_r, sem_c_s, sem_c_r, sem_r_s, sem_r_r, sem_f_s, sem_f_r,
    sem_l_s, sem_l_r, sem_w, sem_y_s, sem_y_r,
):
    p = lax.axis_index("proto")
    y = lax.axis_index("crop")
    chip = p // 2
    core = p % 2
    width, protos = w_raw.shape
    w_copy = pltpu.make_async_copy(w_ref, w_raw, sem_w.at[0])
    w_copy.start()
    crops = e_ref.shape[0]
    n_ct = crops // LANES
    n_pt = protos // LANES
    feat = width // (2 * n_chip)
    n_plane = 2 * n_chip

    bar = pltpu.get_barrier_semaphore()

    def greet_plane(i, c):
        pl.semaphore_signal(bar, inc=1, device_id=(lax.rem(p + i, n_plane), y), device_id_type=MESH)
        return c

    lax.fori_loop(1, n_plane, greet_plane, 0)
    for i in range(1, n_y):
        pl.semaphore_signal(bar, inc=1, device_id=(p, lax.rem(y + i, n_y)), device_id_type=MESH)

    for src, dst in ((t_ref, gt), (s_ref, gs)):
        for j in range(feat):
            for ct in range(n_ct):
                k = n_ct * j + ct
                dst[chip, core, k : k + 1, :] = src[j : j + 1, ct * LANES : (ct + 1) * LANES]

    def prep_w(i, c):
        cols = pl.ds(pl.multiple_of(i * 256, 256), 256)
        w = w_raw[:, cols]
        w = w * (1.0 / jnp.sqrt(jnp.sum(w * w, axis=0, keepdims=True) + EPS))
        hi, lo = split(w)
        w_cat[0:width, cols] = hi
        w_cat[width : 2 * width, cols] = hi
        w_cat[2 * width : 3 * width, cols] = lo
        return c

    w_copy.wait()
    lax.fori_loop(0, protos // 256, prep_w, 0)
    pl.semaphore_wait(bar, n_plane - 1 + n_y - 1)

    def gather_start(buf, k):
        def go(i, c):
            other = lax.rem(chip + i, n_chip)
            pltpu.make_async_remote_copy(
                src_ref=buf.at[chip, core],
                dst_ref=buf.at[chip, core],
                send_sem=sem_g_s.at[k],
                recv_sem=sem_g_r.at[k],
                device_id=(other * 2 + core, y),
                device_id_type=MESH,
            ).start()
            return c

        lax.fori_loop(1, n_chip, go, 0)

    def gather_finish(buf, k):
        await_bytes(buf.at[pl.ds(0, n_chip - 1), core], sem_g_r.at[k])
        await_bytes(buf.at[pl.ds(0, n_chip - 1), core], sem_g_s.at[k])
        cp = pltpu.make_async_remote_copy(
            src_ref=buf.at[:, core],
            dst_ref=buf.at[:, core],
            send_sem=sem_d_s.at[k],
            recv_sem=sem_d_r.at[k],
            device_id=(p + 1 - 2 * core, y),
            device_id_type=MESH,
        )
        cp.start()
        return cp

    def unit(buf, temp, cat, keep):
        flat[...] = buf[...].reshape(flat.shape)
        for ct in range(n_ct):
            rows = pl.ds(ct * LANES, LANES)
            x = flat[pl.ds(ct, width, stride=n_ct), :]
            x = x * (1.0 / jnp.sqrt(jnp.sum(x * x, axis=0, keepdims=True) + EPS))
            if keep:
                hi, lo = split(x)
                zs_hi[:, rows] = hi
                zs_lo[:, rows] = lo
            xt = (x * (1.0 / temp)).T
            hi, lo = split(xt)
            cat[rows, 0:width] = hi
            cat[rows, width : 2 * width] = lo
            cat[rows, 2 * width : 3 * width] = hi

    def col_start(k):
        col_in[k, pl.ds(y, 1)] = col_out[k : k + 1]
        for i in range(1, n_y):
            pltpu.make_async_remote_copy(
                src_ref=col_out.at[k],
                dst_ref=col_in.at[k, y],
                send_sem=sem_c_s.at[k],
                recv_sem=sem_c_r.at[k],
                device_id=(p, lax.rem(y + i, n_y)),
                device_id_type=MESH,
            ).start()

    def col_finish(k):
        await_bytes(col_in.at[k, pl.ds(0, n_y - 1)], sem_c_r.at[k])
        total = col_in[k, 0]
        for i in range(1, n_y):
            total = total + col_in[k, i]
        ubuf[...] = 1.0 / total

    def row_start(k):
        row_in[k, pl.ds(p, 1)] = row_out[k : k + 1]

        def go(i, c):
            pltpu.make_async_remote_copy(
                src_ref=row_out.at[k],
                dst_ref=row_in.at[k, p],
                send_sem=sem_r_s.at[k],
                recv_sem=sem_r_r.at[k],
                device_id=(lax.rem(p + i, n_plane), y),
                device_id_type=MESH,
            ).start()
            return c

        lax.fori_loop(1, n_plane, go, 0)

    def row_finish(k):
        await_bytes(row_in.at[k, pl.ds(0, n_plane - 1)], sem_r_r.at[k])
        return jnp.sum(row_in[k], axis=0)

    def to_rows(k):
        for ct in range(n_ct):
            block = tcol[ct * LANES : (ct + 1) * LANES, :].T
            row_out[k, ct : ct + 1, :] = jnp.sum(block, axis=0, keepdims=True)

    def to_column(values):
        for ct in range(n_ct):
            row = jnp.broadcast_to(values[ct : ct + 1, :], (LANES, LANES))
            vcol[ct * LANES : (ct + 1) * LANES, :] = row.T

    chunk = 64

    def lane_fold(x):
        total = x[:, 0:LANES]
        for j in range(1, n_pt):
            total = total + x[:, j * LANES : (j + 1) * LANES]
        return total

    def scaled_fold(rows, mult):
        total = None
        for j in range(n_pt):
            x = e_ref[rows, j * LANES : (j + 1) * LANES]
            if mult is not None:
                x = x * mult[rows, j * LANES : (j + 1) * LANES]
            x = x * ubuf[j : j + 1, :]
            total = x if total is None else total + x
        return total

    def row_pass(k, mult):
        def go(i, c):
            rows = pl.ds(pl.multiple_of(i * chunk, chunk), chunk)
            tcol[rows, :] = scaled_fold(rows, mult)
            return c

        lax.fori_loop(0, crops // chunk, go, 0)
        to_rows(k)

    def col_pass(k):
        def go(i, acc):
            rows = pl.ds(pl.multiple_of(i * 32, 32), 32)
            v = vcol[rows, :]
            out = []
            for j in range(n_pt):
                x = e_ref[rows, j * LANES : (j + 1) * LANES] * v
                out.append(acc[j] + jnp.sum(x.reshape(4, 8, LANES), axis=0))
            return tuple(out)

        acc = lax.fori_loop(0, crops // 32, go, tuple(jnp.zeros((8, LANES), f32) for _ in range(n_pt)))
        for j in range(n_pt):
            col_out[k, j : j + 1, :] = jnp.sum(acc[j], axis=0, keepdims=True)

    gather_start(gt, 0)
    pair_t = gather_finish(gt, 0)
    gather_start(gs, 1)
    pair_t.wait()
    unit(gt, TEACHER_TEMP, zt_cat, False)

    def teacher_block(i, c):
        cols = pl.ds(pl.multiple_of(i * 256, 256), 256)
        e = jnp.exp(nn(zt_cat[...], w_cat[:, cols]))
        e_ref[:, cols] = e
        sums = jnp.sum(e, axis=0, keepdims=True)
        col_out[0, pl.ds(2 * i, 1), :] = sums[:, 0:LANES]
        col_out[0, pl.ds(2 * i + 1, 1), :] = sums[:, LANES : 2 * LANES]
        return c

    lax.fori_loop(0, protos // 256, teacher_block, 0)
    col_start(0)
    col_finish(0)
    row_pass(0, None)
    row_start(0)

    gather_finish(gs, 1).wait()
    unit(gs, STUDENT_TEMP, zs_cat, True)

    def student_block(i, c):
        cols = pl.ds(pl.multiple_of(i * 256, 256), 256)
        s = nn(zs_cat[...], w_cat[:, cols])
        s_log[:, cols] = s
        es_ref[:, cols] = jnp.exp(s)
        return c

    lax.fori_loop(0, protos // 256, student_block, 0)
    for k in (1, 2):
        to_column(1.0 / row_finish(k - 1))
        col_pass(k)
        col_start(k)
        if k == 1:
            def fold(i, c):
                rows = pl.ds(pl.multiple_of(i * chunk, chunk), chunk)
                tcol[rows, :] = lane_fold(es_ref[rows, :])
                return c

            lax.fori_loop(0, crops // chunk, fold, 0)
            to_rows(3)
            row_start(3)
        col_finish(k)
        row_pass(k, None)
        row_start(k)
    row_pass(4, s_log)
    row_start(4)
    last = row_finish(2)
    student_total = row_finish(3)
    to_column(scale / last)
    tv = scale / student_total
    for ct in range(n_ct):
        row = jnp.broadcast_to(tv[ct : ct + 1, :], (LANES, LANES))
        tcol[ct * LANES : (ct + 1) * LANES, :] = row.T

    ahead = lax.rem(y + 1, n_y)
    across = lax.rem(y + 2, n_y)
    behind = lax.rem(y + n_y - 1, n_y)
    out_rows = width // n_y
    half = 256
    n_part = protos // (2 * half)

    def rows_of(d):
        return pl.ds(pl.multiple_of(d * out_rows, 8), out_rows)

    def hop(src, dst, s, r, target):
        pltpu.make_async_remote_copy(
            src_ref=src, dst_ref=dst, send_sem=s, recv_sem=r, device_id=(p, target), device_id_type=MESH
        ).start()

    def proto_part(i):
        base = i * 2 * half

        def grad_block(r, c):
            rows = pl.ds(pl.multiple_of(r * 64, 64), 64)
            v = vcol[rows, :]
            t = tcol[rows, :]
            for j in range(2 * half // LANES):
                lanes = slice(base + j * LANES, base + (j + 1) * LANES)
                k = base // LANES + j
                g = es_ref[rows, lanes] * t - e_ref[rows, lanes] * ubuf[k : k + 1, :] * v
                hi, lo = split(g)
                g_hi[rows, lanes] = hi
                g_lo[rows, lanes] = lo
            return c

        lax.fori_loop(0, crops // 64, grad_block, 0)
        for h in range(2):
            lanes = slice(base + h * half, base + (h + 1) * half)
            a = g_hi[:, lanes]
            part[i, h] = nn(zs_hi[...], a) + nn(zs_lo[...], a) + nn(zs_hi[...], g_lo[:, lanes])
        hop(part.at[i, 0, rows_of(across)], relay.at[i, 0], sem_y_s.at[i, 0], sem_y_r.at[i, 0], ahead)
        hop(part.at[i, 1, rows_of(across)], relay.at[i, 1], sem_y_s.at[i, 1], sem_y_r.at[i, 1], behind)
        hop(part.at[i, 1, rows_of(ahead)], final.at[i, 0, 1], sem_y_s.at[i, 2], sem_y_r.at[i, 2], ahead)
        hop(part.at[i, 0, rows_of(behind)], final.at[i, 1, 0], sem_y_s.at[i, 3], sem_y_r.at[i, 3], behind)

    def relay_part(i):
        await_bytes(relay.at[i, 0], sem_y_r.at[i, 0])
        relay[i, 0] += part[i, 0, rows_of(ahead)]
        hop(relay.at[i, 0], final.at[i, 0, 0], sem_y_s.at[i, 4], sem_y_r.at[i, 2], ahead)
        await_bytes(relay.at[i, 1], sem_y_r.at[i, 1])
        relay[i, 1] += part[i, 1, rows_of(behind)]
        hop(relay.at[i, 1], final.at[i, 1, 1], sem_y_s.at[i, 5], sem_y_r.at[i, 3], behind)

    def final_part(i):
        for side in range(2):
            await_bytes(final.at[i, side], sem_y_r.at[i, 2 + side])
        for h in range(2):
            lanes = slice((2 * i + h) * half, (2 * i + h + 1) * half)
            gp_ref[:, lanes] = part[i, h, rows_of(y)] + final[i, 0, h] + final[i, 1, h]

    for i in range(n_part):
        proto_part(i)

    gf_acc[...] = jnp.zeros_like(gf_acc)

    def feat_block(i, c):
        cols = pl.ds(pl.multiple_of(i * 512, 512), 512)
        w_hi = w_cat[0:width, cols]
        w_lo = w_cat[2 * width : 3 * width, cols]
        gf_acc[...] += nt(w_hi, g_hi[:, cols]) + nt(w_hi, g_lo[:, cols]) + nt(w_lo, g_hi[:, cols])
        return c

    lax.fori_loop(0, protos // 512, feat_block, 0)
    for ct in range(n_ct):
        rs_flat[pl.ds(ct, width, stride=n_ct), :] = gf_acc[:, ct * LANES : (ct + 1) * LANES]
    rs_src[...] = rs_flat[...].reshape(rs_src.shape)
    pair = pltpu.make_async_remote_copy(
        src_ref=rs_src.at[:, 1 - core],
        dst_ref=rs_pair,
        send_sem=sem_f_s.at[0],
        recv_sem=sem_f_r.at[0],
        device_id=(p + 1 - 2 * core, y),
        device_id_type=MESH,
    )
    pair.start()
    relay_part(0)
    pair.wait()
    rs_pair[...] += rs_src[:, core]
    rs_in[pl.ds(chip, 1)] = rs_pair[pl.ds(chip, 1)]

    def scatter(i, c):
        other = lax.rem(chip + i, n_chip)
        pltpu.make_async_remote_copy(
            src_ref=rs_pair.at[other],
            dst_ref=rs_in.at[chip],
            send_sem=sem_f_s.at[1],
            recv_sem=sem_f_r.at[1],
            device_id=(other * 2 + core, y),
            device_id_type=MESH,
        ).start()
        return c

    lax.fori_loop(1, n_chip, scatter, 0)
    for i in range(1, n_part):
        relay_part(i)
    cross = row_finish(4)
    loss_in[pl.ds(y, 1)] = (jnp.log(student_total) - cross / last)[None]
    for i in range(1, n_y):
        hop(loss_in.at[y], loss_in.at[y], sem_l_s.at[0], sem_l_r.at[0], lax.rem(y + i, n_y))

    await_bytes(rs_in.at[pl.ds(0, n_chip - 1)], sem_f_r.at[1])
    total = jnp.sum(rs_in[...], axis=0)
    for j in range(feat):
        for ct in range(n_ct):
            k = n_ct * j + ct
            gf_ref[j : j + 1, ct * LANES : (ct + 1) * LANES] = total[k : k + 1, :]
    for i in range(n_part):
        final_part(i)
    await_bytes(loss_in.at[pl.ds(0, n_y - 1)], sem_l_r.at[0])
    loss_ref[0, 0] = jnp.sum(jnp.sum(loss_in[...], axis=0)) * (1.0 / crops_all)

    for i in range(n_part):
        for k in range(6):
            await_bytes(relay.at[i, 0], sem_y_s.at[i, k])
    await_bytes(loss_in.at[pl.ds(0, n_y - 1)], sem_l_s.at[0])
    await_bytes(rs_in.at[pl.ds(0, n_chip - 1)], sem_f_s.at[1])
    for k in range(3):
        await_bytes(col_in.at[k, pl.ds(0, n_y - 1)], sem_c_s.at[k])
    for k in range(5):
        await_bytes(row_in.at[k, pl.ds(0, n_plane - 1)], sem_r_s.at[k])


def on_device(n_y, n_chip, t, s, w):
    width, protos = w.shape
    feat, crops = t.shape
    n_ct = crops // LANES
    n_pt = protos // LANES
    n_plane = 2 * n_chip
    scale = math.sqrt(protos * n_plane) / STUDENT_TEMP
    vm = pltpu.VMEM
    dma = pltpu.SemaphoreType.DMA
    slots = (n_chip, 2, feat * n_ct, LANES)
    gf, gp, loss = pl.pallas_call(
        functools.partial(kernel, n_y, n_chip, scale, crops * n_y),
        out_shape=(
            jax.ShapeDtypeStruct((feat, crops), f32),
            jax.ShapeDtypeStruct((width // n_y, protos), f32),
            jax.ShapeDtypeStruct((1, 1), f32),
        ),
        in_specs=[
            pl.BlockSpec(memory_space=vm),
            pl.BlockSpec(memory_space=vm),
            pl.BlockSpec(memory_space=pl.ANY),
        ],
        out_specs=(
            pl.BlockSpec(memory_space=vm),
            pl.BlockSpec(memory_space=vm),
            pl.BlockSpec(memory_space=pltpu.SMEM),
        ),
        scratch_shapes=[
            vm(slots, f32),
            vm(slots, f32),
            vm((width * n_ct, LANES), f32),
            vm((crops, 3 * width), bf16),
            vm((crops, 3 * width), bf16),
            vm((width, crops), bf16),
            vm((width, crops), bf16),
            vm((3 * width, protos), bf16),
            vm((crops, protos), f32),
            vm((crops, protos), f32),
            vm((crops, protos), f32),
            vm((crops, protos), bf16),
            vm((crops, protos), bf16),
            vm((crops, LANES), f32),
            vm((crops, LANES), f32),
            vm((3, n_pt, LANES), f32),
            vm((3, n_y, n_pt, LANES), f32),
            vm((n_pt, LANES), f32),
            vm((5, n_ct, LANES), f32),
            vm((5, n_plane, n_ct, LANES), f32),
            vm((width, crops), f32),
            vm((width * n_ct, LANES), f32),
            vm(slots, f32),
            vm((n_chip, feat * n_ct, LANES), f32),
            vm((n_chip, feat * n_ct, LANES), f32),
            vm((n_y, n_ct, LANES), f32),
            vm((width, protos), f32),
            vm((protos // 512, 2, width, 256), f32),
            vm((protos // 512, 2, width // n_y, 256), f32),
            vm((protos // 512, 2, 2, width // n_y, 256), f32),
            dma((2,)), dma((2,)), dma((2,)), dma((2,)), dma((3,)), dma((3,)), dma((5,)), dma((5,)),
            dma((2,)), dma((2,)), dma((1,)), dma((1,)),
            dma((1,)), dma((protos // 512, 6)), dma((protos // 512, 4)),
        ],
        compiler_params=pltpu.CompilerParams(
            collective_id=0, has_side_effects=True, vmem_limit_bytes=60 * 2**20
        ),
    )(t, s, w)
    return gf, gp, loss.reshape(())


def solution(mesh):
    placed = (P("proto", "crop"), P("proto", "crop"), P(None, "proto"))
    n_y = mesh.shape["crop"]
    n_chip = mesh.shape["proto"] // 2
    return jax.shard_map(
        functools.partial(on_device, n_y, n_chip),
        mesh=mesh,
        in_specs=placed,
        out_specs=(P("proto", "crop"), P("crop", "proto"), P()),
        check_vma=False,
    )
```

```python
import functools
import math

import jax
import jax.numpy as jnp
from jax import lax
from jax.experimental import pallas as pl
from jax.experimental.pallas import tpu as pltpu
from jax.sharding import PartitionSpec as P

MESH = pl.DeviceIdType.MESH
TEACHER_TEMP = 0.07
STUDENT_TEMP = 0.1
EPS = 1e-06
ITERS = 3
f32 = jnp.float32
bf16 = jnp.bfloat16
LANES = 128


def split(x):
    hi = x.astype(bf16)
    return hi, (x - hi.astype(f32)).astype(bf16)


def await_bytes(ref, sem):
    pltpu.make_async_copy(ref, ref, sem).wait()


def nn(a, b):
    return lax.dot_general(a, b, (((1,), (0,)), ((), ())), preferred_element_type=f32)


def nt(a, b):
    return lax.dot_general(a, b, (((1,), (1,)), ((), ())), preferred_element_type=f32)


def kernel(
    n_y, n_chip, scale, crops_all,
    t_ref, s_ref, w_ref,
    gf_ref, gp_ref, loss_ref,
    gt, gs, flat, zt_cat, zs_cat, zs_hi, zs_lo, w_cat, e_ref, s_log, es_ref, g_hi, g_lo,
    er, esr, gr_hi, gr_lo, far, vfar, tfar,
    tcol, vcol, col_out, col_in, ubuf, row_out, row_in, gf_acc, rs_flat, rs_src, rs_pair, rs_in,
    loss_in, w_raw, part, final,
    sem_g_s, sem_g_r, sem_d_s, sem_d_r, sem_c_s, sem_c_r, sem_r_s, sem_r_r, sem_f_s, sem_f_r,
    sem_l_s, sem_l_r, sem_w, sem_y_s, sem_y_r, sem_a_s, sem_a_r,
    sem_e_s, sem_e_r, sem_v_s, sem_v_r,
):
    p = lax.axis_index("proto")
    y = lax.axis_index("crop")
    chip = p // 2
    core = p % 2
    width, protos = w_raw.shape
    w_copy = pltpu.make_async_copy(w_ref, w_raw, sem_w.at[0])
    w_copy.start()
    crops = e_ref.shape[0]
    n_ct = crops // LANES
    n_pt = protos // LANES
    feat = width // (2 * n_chip)
    n_plane = 2 * n_chip
    n_z = 8
    n_x = n_chip // n_z
    chip_x = chip // n_z
    chip_z = chip % n_z
    groups = (0, 1, 3, 2)
    ahead = lax.rem(y + 1, n_y)
    across = lax.rem(y + 2, n_y)
    behind = lax.rem(y + n_y - 1, n_y)
    mine = protos // n_y

    bar = pltpu.get_barrier_semaphore()

    def greet_plane(i, c):
        pl.semaphore_signal(bar, inc=1, device_id=(lax.rem(p + i, n_plane), y), device_id_type=MESH)
        return c

    lax.fori_loop(1, n_plane, greet_plane, 0)
    for i in range(1, n_y):
        pl.semaphore_signal(bar, inc=1, device_id=(p, lax.rem(y + i, n_y)), device_id_type=MESH)

    for src, dst in ((t_ref, gt), (s_ref, gs)):
        for j in range(feat):
            for ct in range(n_ct):
                k = n_ct * j + ct
                dst[0, chip, core, k : k + 1, :] = src[j : j + 1, ct * LANES : (ct + 1) * LANES]

    def prep_w(i, c):
        cols = pl.ds(pl.multiple_of(i * 256, 256), 256)
        w = w_raw[:, cols]
        w = w * (1.0 / jnp.sqrt(jnp.sum(w * w, axis=0, keepdims=True) + EPS))
        hi, lo = split(w)
        w_cat[0:width, cols] = hi
        w_cat[width : 2 * width, cols] = hi
        w_cat[2 * width : 3 * width, cols] = lo
        return c

    w_copy.wait()
    lax.fori_loop(0, protos // 256, prep_w, 0)
    pl.semaphore_wait(bar, n_plane - 1 + n_y - 1)

    def remote(src, dst, s, r, plane, crop):
        copy = pltpu.make_async_remote_copy(
            src_ref=src, dst_ref=dst, send_sem=s, recv_sem=r, device_id=(plane, crop), device_id_type=MESH
        )
        copy.start()
        return copy

    sibling = p + 1 - 2 * core

    def gather_start(buf, k):
        for dx in groups:
            def go(dz, c):
                other = lax.rem(chip_x + dx, n_x) * n_z + lax.rem(chip_z + dz, n_z)
                here = buf.at[0, chip, core]
                remote(here, here, sem_g_s.at[k], sem_g_r.at[k, dx], other * 2 + core, y)
                return c

            lax.fori_loop(1 if dx == 0 else 0, n_z, go, 0)

    def slots_of(dx):
        return pl.ds(pl.multiple_of(lax.rem(chip_x + n_x - dx, n_x) * n_z, n_z), n_z)

    def gather_group(buf, k, dx):
        got = buf.at[0, pl.ds(0, n_z - 1 if dx == 0 else n_z), core]
        await_bytes(got, sem_g_r.at[k, dx])
        block = buf.at[0, slots_of(dx), core]
        remote(block, block, sem_d_s.at[k], sem_d_r.at[k], sibling, y)

    def spread_group(buf, k, dx):
        block = buf.at[0, slots_of(dx), core]
        remote(block, buf.at[n_y - 1, slots_of(dx), core], sem_a_s.at[k, 0], sem_a_r.at[k, 0], p, ahead)
        remote(block, buf.at[1, slots_of(dx), core], sem_a_s.at[k, 1], sem_a_r.at[k, 1], p, behind)

    def gather_finish(buf, k):
        await_bytes(buf.at[0, :, core], sem_d_r.at[k])

    def share(buf, k, rel):
        block = buf.at[rel, :, core]
        remote(block, block, sem_e_s.at[k, rel - 1], sem_e_r.at[k, rel - 1], sibling, y)

    def near_finish(buf, k):
        await_bytes(buf.at[n_y - 1, :, core], sem_a_r.at[k, 0])
        await_bytes(buf.at[1, :, core], sem_a_r.at[k, 1])
        share(buf, k, 1)
        share(buf, k, 3)

    def relay(buf, k):
        low, high = pl.ds(0, n_chip // 2), pl.ds(n_chip // 2, n_chip // 2)
        remote(buf.at[3, low, core], buf.at[2, low, core], sem_a_s.at[k, 2], sem_a_r.at[k, 2], p, ahead)
        remote(buf.at[1, high, core], buf.at[2, high, core], sem_a_s.at[k, 3], sem_a_r.at[k, 3], p, behind)

    def far_finish(buf, k):
        for i in (2, 3):
            await_bytes(buf.at[2, pl.ds(0, n_chip // 2), core], sem_a_r.at[k, i])
        share(buf, k, 2)

    def unit(buf, rel, temp, cat, keep):
        flat[...] = buf[rel].reshape(flat.shape)
        for ct in range(n_ct):
            rows = pl.ds(ct * LANES, LANES)
            x = flat[pl.ds(ct, width, stride=n_ct), :]
            x = x * (1.0 / jnp.sqrt(jnp.sum(x * x, axis=0, keepdims=True) + EPS))
            if keep:
                hi, lo = split(x)
                zs_hi[rel, :, rows] = hi
                zs_lo[rel, :, rows] = lo
            xt = (x * (1.0 / temp)).T
            hi, lo = split(xt)
            cat[rows, 0:width] = hi
            cat[rows, width : 2 * width] = lo
            cat[rows, 2 * width : 3 * width] = hi

    def other_block(buf, k, rel, temp, dst, keep):
        await_bytes(buf.at[rel, :, core], sem_e_r.at[k, rel - 1])
        unit(buf, rel, temp, zt_cat, keep)
        for h in range(mine // 256):
            cols = pl.ds(pl.multiple_of(y * mine + h * 256, 256), 256)
            dst[rel - 1, :, h * 256 : (h + 1) * 256] = jnp.exp(nn(zt_cat[...], w_cat[:, cols]))

    def col_start(k):
        col_in[k, pl.ds(y, 1)] = col_out[k : k + 1]
        for i in range(1, n_y):
            pltpu.make_async_remote_copy(
                src_ref=col_out.at[k],
                dst_ref=col_in.at[k, y],
                send_sem=sem_c_s.at[k],
                recv_sem=sem_c_r.at[k],
                device_id=(p, lax.rem(y + i, n_y)),
                device_id_type=MESH,
            ).start()

    def col_finish(k):
        await_bytes(col_in.at[k, pl.ds(0, n_y - 1)], sem_c_r.at[k])
        total = col_in[k, 0]
        for i in range(1, n_y):
            total = total + col_in[k, i]
        ubuf[...] = 1.0 / total

    def row_start(k):
        row_in[k, pl.ds(p, 1)] = row_out[k : k + 1]

        def go(i, c):
            pltpu.make_async_remote_copy(
                src_ref=row_out.at[k],
                dst_ref=row_in.at[k, p],
                send_sem=sem_r_s.at[k],
                recv_sem=sem_r_r.at[k],
                device_id=(lax.rem(p + i, n_plane), y),
                device_id_type=MESH,
            ).start()
            return c

        lax.fori_loop(1, n_plane, go, 0)

    def row_finish(k):
        await_bytes(row_in.at[k, pl.ds(0, n_plane - 1)], sem_r_r.at[k])
        return jnp.sum(row_in[k], axis=0)

    def to_rows(k):
        for ct in range(n_ct):
            block = tcol[ct * LANES : (ct + 1) * LANES, :].T
            row_out[k, ct : ct + 1, :] = jnp.sum(block, axis=0, keepdims=True)

    def to_column(values):
        for ct in range(n_ct):
            row = jnp.broadcast_to(values[ct : ct + 1, :], (LANES, LANES))
            vcol[ct * LANES : (ct + 1) * LANES, :] = row.T

    chunk = 64

    def lane_fold(x):
        total = x[:, 0:LANES]
        for j in range(1, n_pt):
            total = total + x[:, j * LANES : (j + 1) * LANES]
        return total

    def scaled_fold(rows, mult):
        total = None
        for j in range(n_pt):
            x = e_ref[rows, j * LANES : (j + 1) * LANES]
            if mult is not None:
                x = x * mult[rows, j * LANES : (j + 1) * LANES]
            x = x * ubuf[j : j + 1, :]
            total = x if total is None else total + x
        return total

    def row_pass(k, mult):
        def go(i, c):
            rows = pl.ds(pl.multiple_of(i * chunk, chunk), chunk)
            tcol[rows, :] = scaled_fold(rows, mult)
            return c

        lax.fori_loop(0, crops // chunk, go, 0)
        to_rows(k)

    def col_pass(k):
        def go(i, acc):
            rows = pl.ds(pl.multiple_of(i * 32, 32), 32)
            v = vcol[rows, :]
            out = []
            for j in range(n_pt):
                x = e_ref[rows, j * LANES : (j + 1) * LANES] * v
                out.append(acc[j] + jnp.sum(x.reshape(4, 8, LANES), axis=0))
            return tuple(out)

        acc = lax.fori_loop(0, crops // 32, go, tuple(jnp.zeros((8, LANES), f32) for _ in range(n_pt)))
        for j in range(n_pt):
            col_out[k, j : j + 1, :] = jnp.sum(acc[j], axis=0, keepdims=True)

    gather_start(gt, 0)
    for dx in groups:
        gather_group(gt, 0, dx)
        spread_group(gt, 0, dx)
    gather_start(gs, 1)
    gather_finish(gt, 0)
    unit(gt, 0, TEACHER_TEMP, zt_cat, False)

    def teacher_block(i, c):
        cols = pl.ds(pl.multiple_of(i * 256, 256), 256)
        e = jnp.exp(nn(zt_cat[...], w_cat[:, cols]))
        e_ref[:, cols] = e
        sums = jnp.sum(e, axis=0, keepdims=True)
        col_out[0, pl.ds(2 * i, 1), :] = sums[:, 0:LANES]
        col_out[0, pl.ds(2 * i + 1, 1), :] = sums[:, LANES : 2 * LANES]
        return c

    lax.fori_loop(0, protos // 256, teacher_block, 0)
    col_start(0)
    near_finish(gt, 0)
    col_finish(0)
    row_pass(0, None)
    row_start(0)
    relay(gt, 0)

    for dx in groups:
        gather_group(gs, 1, dx)
    spread_group(gs, 1, 0)
    gather_finish(gs, 1)
    unit(gs, 0, STUDENT_TEMP, zs_cat, True)

    def student_block(i, c):
        cols = pl.ds(pl.multiple_of(i * 256, 256), 256)
        s = nn(zs_cat[...], w_cat[:, cols])
        s_log[:, cols] = s
        es_ref[:, cols] = jnp.exp(s)
        return c

    lax.fori_loop(0, protos // 256, student_block, 0)
    for k in (1, 2):
        to_column(1.0 / row_finish(k - 1))
        col_pass(k)
        col_start(k)
        if k == 1:
            def fold(i, c):
                rows = pl.ds(pl.multiple_of(i * chunk, chunk), chunk)
                tcol[rows, :] = lane_fold(es_ref[rows, :])
                return c

            lax.fori_loop(0, crops // chunk, fold, 0)
            to_rows(3)
            row_start(3)
            other_block(gt, 0, 1, TEACHER_TEMP, er, False)
            far_finish(gt, 0)
        else:
            near_finish(gs, 1)
        col_finish(k)
        row_pass(k, None)
        row_start(k)
        if k == 1:
            for dx in groups[1:]:
                spread_group(gs, 1, dx)
            other_block(gt, 0, 3, TEACHER_TEMP, er, False)
            other_block(gt, 0, 2, TEACHER_TEMP, er, False)
        else:
            relay(gs, 1)
    row_pass(4, s_log)
    row_start(4)
    other_block(gs, 1, 1, STUDENT_TEMP, esr, True)
    other_block(gs, 1, 3, STUDENT_TEMP, esr, True)
    last = row_finish(2)
    student_total = row_finish(3)
    far[0, 0:n_ct, :] = scale / last
    far[0, n_ct : 2 * n_ct, :] = scale / student_total
    for i in range(1, n_y):
        remote(far.at[0], far.at[n_y - i], sem_v_s.at[0], sem_v_r.at[0], p, lax.rem(y + i, n_y))

    def spread_columns(rel, v_dst, t_dst):
        for ct in range(n_ct):
            rows = slice(ct * LANES, (ct + 1) * LANES)
            for dst, k in ((v_dst, ct), (t_dst, n_ct + ct)):
                row = jnp.broadcast_to(far[rel, k : k + 1, :], (LANES, LANES))
                dst[rows, :] = row.T

    spread_columns(0, vcol, tcol)

    def grad_block(r, c):
        rows = pl.ds(pl.multiple_of(r * 32, 32), 32)
        v = vcol[rows, :]
        t = tcol[rows, :]
        for j in range(n_pt):
            lanes = slice(j * LANES, (j + 1) * LANES)
            g = es_ref[rows, lanes] * t - e_ref[rows, lanes] * ubuf[j : j + 1, :] * v
            hi, lo = split(g)
            g_hi[rows, lanes] = hi
            g_lo[rows, lanes] = lo
        return c

    lax.fori_loop(0, crops // 32, grad_block, 0)

    gf_acc[...] = jnp.zeros_like(gf_acc)

    def feat_block(i, c):
        cols = pl.ds(pl.multiple_of(i * 512, 512), 512)
        w_hi = w_cat[0:width, cols]
        w_lo = w_cat[2 * width : 3 * width, cols]
        gf_acc[...] += nt(w_hi, g_hi[:, cols]) + nt(w_hi, g_lo[:, cols]) + nt(w_lo, g_hi[:, cols])
        return c

    lax.fori_loop(0, protos // 512, feat_block, 0)
    for ct in range(n_ct):
        rs_flat[pl.ds(ct, width, stride=n_ct), :] = gf_acc[:, ct * LANES : (ct + 1) * LANES]
    rs_src[...] = rs_flat[...].reshape(rs_src.shape)
    pair = pltpu.make_async_remote_copy(
        src_ref=rs_src.at[:, 1 - core],
        dst_ref=rs_pair,
        send_sem=sem_f_s.at[0],
        recv_sem=sem_f_r.at[0],
        device_id=(p + 1 - 2 * core, y),
        device_id_type=MESH,
    )
    pair.start()
    cross = row_finish(4)
    loss_in[pl.ds(y, 1)] = (jnp.log(student_total) - cross / last)[None]
    for i in range(1, n_y):
        remote(loss_in.at[y], loss_in.at[y], sem_l_s.at[0], sem_l_r.at[0], p, lax.rem(y + i, n_y))
    far_finish(gs, 1)
    pair.wait()
    rs_pair[...] += rs_src[:, core]
    rs_in[pl.ds(chip, 1)] = rs_pair[pl.ds(chip, 1)]

    def scatter(i, c):
        other = lax.rem(chip + i, n_chip)
        pltpu.make_async_remote_copy(
            src_ref=rs_pair.at[other],
            dst_ref=rs_in.at[chip],
            send_sem=sem_f_s.at[1],
            recv_sem=sem_f_r.at[1],
            device_id=(other * 2 + core, y),
            device_id_type=MESH,
        ).start()
        return c

    lax.fori_loop(1, n_chip, scatter, 0)
    other_block(gs, 1, 2, STUDENT_TEMP, esr, True)
    await_bytes(far.at[pl.ds(1, n_y - 1)], sem_v_r.at[0])
    for rel in range(1, n_y):
        spread_columns(rel, vfar.at[rel - 1], tfar.at[rel - 1])

    out_rows = width // n_y
    half = 256

    def rows_of(d):
        return pl.ds(pl.multiple_of(d * out_rows, 8), out_rows)

    def proto_part(h):
        base = pl.multiple_of(y * mine + h * half, half)
        lanes_r = slice(h * half, (h + 1) * half)
        own = pl.ds(base, half)
        for rel in range(1, n_y):
            def go(r, c):
                rows = pl.ds(pl.multiple_of(r * 64, 64), 64)
                v = vfar[rel - 1, rows, :]
                t = tfar[rel - 1, rows, :]
                for j in range(half // LANES):
                    lanes = slice(h * half + j * LANES, h * half + (j + 1) * LANES)
                    u = ubuf[pl.ds(y * (mine // LANES) + h * (half // LANES) + j, 1), :]
                    g = esr[rel - 1, rows, lanes] * t - er[rel - 1, rows, lanes] * u * v
                    hi, lo = split(g)
                    gr_hi[rel - 1, rows, lanes] = hi
                    gr_lo[rel - 1, rows, lanes] = lo
                return c

            lax.fori_loop(0, crops // 64, go, 0)
        total = None
        for rel in range(n_y):
            if rel == 0:
                a, b = g_hi[:, own], g_lo[:, own]
            else:
                a, b = gr_hi[rel - 1, :, lanes_r], gr_lo[rel - 1, :, lanes_r]
            piece = nn(zs_hi[rel], a) + nn(zs_lo[rel], a) + nn(zs_hi[rel], b)
            total = piece if total is None else total + piece
        part[h] = total
        final[h, pl.ds(y, 1)] = part[h, rows_of(y)][None]
        for i in range(1, n_y):
            to = lax.rem(y + i, n_y)
            remote(part.at[h, rows_of(to)], final.at[h, y], sem_y_s.at[h], sem_y_r.at[h], p, to)

    for h in range(mine // half):
        proto_part(h)

    await_bytes(rs_in.at[pl.ds(0, n_chip - 1)], sem_f_r.at[1])
    total = jnp.sum(rs_in[...], axis=0)
    for j in range(feat):
        for ct in range(n_ct):
            k = n_ct * j + ct
            gf_ref[j : j + 1, ct * LANES : (ct + 1) * LANES] = total[k : k + 1, :]
    for h in range(mine // half):
        await_bytes(final.at[h, pl.ds(0, n_y - 1)], sem_y_r.at[h])
        for q in range(n_y):
            gp_ref[:, q * mine + h * half : q * mine + (h + 1) * half] = final[h, q]
    await_bytes(loss_in.at[pl.ds(0, n_y - 1)], sem_l_r.at[0])
    loss_ref[0, 0] = jnp.sum(jnp.sum(loss_in[...], axis=0)) * (1.0 / crops_all)

    for k, buf in ((0, gt), (1, gs)):
        await_bytes(buf.at[0, pl.ds(0, n_chip - 1), core], sem_g_s.at[k])
        await_bytes(buf.at[0, :, core], sem_d_s.at[k])
        for i in range(2):
            await_bytes(buf.at[0, :, core], sem_a_s.at[k, i])
            await_bytes(buf.at[0, pl.ds(0, n_chip // 2), core], sem_a_s.at[k, 2 + i])
        for i in range(n_y - 1):
            await_bytes(buf.at[0, :, core], sem_e_s.at[k, i])
    await_bytes(far.at[pl.ds(1, n_y - 1)], sem_v_s.at[0])
    for h in range(mine // half):
        await_bytes(final.at[h, pl.ds(0, n_y - 1)], sem_y_s.at[h])
    await_bytes(loss_in.at[pl.ds(0, n_y - 1)], sem_l_s.at[0])
    await_bytes(rs_in.at[pl.ds(0, n_chip - 1)], sem_f_s.at[1])
    for k in range(3):
        await_bytes(col_in.at[k, pl.ds(0, n_y - 1)], sem_c_s.at[k])
    for k in range(5):
        await_bytes(row_in.at[k, pl.ds(0, n_plane - 1)], sem_r_s.at[k])


def on_device(n_y, n_chip, t, s, w):
    width, protos = w.shape
    feat, crops = t.shape
    n_ct = crops // LANES
    n_pt = protos // LANES
    n_plane = 2 * n_chip
    scale = math.sqrt(protos * n_plane) / STUDENT_TEMP
    vm = pltpu.VMEM
    dma = pltpu.SemaphoreType.DMA
    slots = (n_chip, 2, feat * n_ct, LANES)
    mine = protos // n_y
    gf, gp, loss = pl.pallas_call(
        functools.partial(kernel, n_y, n_chip, scale, crops * n_y),
        out_shape=(
            jax.ShapeDtypeStruct((feat, crops), f32),
            jax.ShapeDtypeStruct((width // n_y, protos), f32),
            jax.ShapeDtypeStruct((1, 1), f32),
        ),
        in_specs=[
            pl.BlockSpec(memory_space=vm),
            pl.BlockSpec(memory_space=vm),
            pl.BlockSpec(memory_space=pl.ANY),
        ],
        out_specs=(
            pl.BlockSpec(memory_space=vm),
            pl.BlockSpec(memory_space=vm),
            pl.BlockSpec(memory_space=pltpu.SMEM),
        ),
        scratch_shapes=[
            vm((n_y,) + slots, f32),
            vm((n_y,) + slots, f32),
            vm((width * n_ct, LANES), f32),
            vm((crops, 3 * width), bf16),
            vm((crops, 3 * width), bf16),
            vm((n_y, width, crops), bf16),
            vm((n_y, width, crops), bf16),
            vm((3 * width, protos), bf16),
            vm((crops, protos), f32),
            vm((crops, protos), f32),
            vm((crops, protos), f32),
            vm((crops, protos), bf16),
            vm((crops, protos), bf16),
            vm((n_y - 1, crops, mine), f32),
            vm((n_y - 1, crops, mine), f32),
            vm((n_y - 1, crops, mine), bf16),
            vm((n_y - 1, crops, mine), bf16),
            vm((n_y, 2 * n_ct, LANES), f32),
            vm((n_y - 1, crops, LANES), f32),
            vm((n_y - 1, crops, LANES), f32),
            vm((crops, LANES), f32),
            vm((crops, LANES), f32),
            vm((3, n_pt, LANES), f32),
            vm((3, n_y, n_pt, LANES), f32),
            vm((n_pt, LANES), f32),
            vm((5, n_ct, LANES), f32),
            vm((5, n_plane, n_ct, LANES), f32),
            vm((width, crops), f32),
            vm((width * n_ct, LANES), f32),
            vm(slots, f32),
            vm((n_chip, feat * n_ct, LANES), f32),
            vm((n_chip, feat * n_ct, LANES), f32),
            vm((n_y, n_ct, LANES), f32),
            vm((width, protos), f32),
            vm((mine // 256, width, 256), f32),
            vm((mine // 256, n_y, width // n_y, 256), f32),
            dma((2,)), dma((2, 4)), dma((2,)), dma((2,)), dma((3,)), dma((3,)), dma((5,)), dma((5,)),
            dma((2,)), dma((2,)), dma((1,)), dma((1,)),
            dma((1,)), dma((mine // 256,)), dma((mine // 256,)), dma((2, 4)), dma((2, 4)),
            dma((2, 3)), dma((2, 3)), dma((1,)), dma((1,)),
        ],
        compiler_params=pltpu.CompilerParams(
            collective_id=0, has_side_effects=True, vmem_limit_bytes=60 * 2**20
        ),
    )(t, s, w)
    return gf, gp, loss.reshape(())


def solution(mesh):
    placed = (P("proto", "crop"), P("proto", "crop"), P(None, "proto"))
    n_y = mesh.shape["crop"]
    n_chip = mesh.shape["proto"] // 2
    return jax.shard_map(
        functools.partial(on_device, n_y, n_chip),
        mesh=mesh,
        in_specs=placed,
        out_specs=(P("proto", "crop"), P("crop", "proto"), P()),
        check_vma=False,
    )
```

```python
import functools
import math

import jax
import jax.numpy as jnp
from jax import lax
from jax.experimental import pallas as pl
from jax.experimental.pallas import tpu as pltpu
from jax.sharding import PartitionSpec as P

MESH = pl.DeviceIdType.MESH
TEACHER_TEMP = 0.07
STUDENT_TEMP = 0.1
EPS = 1e-06
ITERS = 3
f32 = jnp.float32
bf16 = jnp.bfloat16
LANES = 128


def split(x):
    hi = x.astype(bf16)
    return hi, (x - hi.astype(f32)).astype(bf16)


def await_bytes(ref, sem):
    pltpu.make_async_copy(ref, ref, sem).wait()


def nn(a, b):
    return lax.dot_general(a, b, (((1,), (0,)), ((), ())), preferred_element_type=f32)


def nt(a, b):
    return lax.dot_general(a, b, (((1,), (1,)), ((), ())), preferred_element_type=f32)


def kernel(
    n_y, n_chip, scale, crops_all,
    t_ref, s_ref, w_ref,
    gf_ref, gp_ref, loss_ref,
    gt, gs, flat, zt_cat, zs_cat, z_cat, w_cat, e_ref, s_log, es_ref, g_hi, g_lo,
    er, esr, g_cat, far, vfar, tfar, a1, a2,
    tcol, vcol, col_out, col_in, ubuf, row_out, row_in, rs_flat, rs_src, rs_pair, rs_in,
    loss_in, part, final,
    sem_g_s, sem_g_r, sem_d_s, sem_d_r, sem_c_s, sem_c_r, sem_r_s, sem_r_r, sem_f_s, sem_f_r,
    sem_l_s, sem_l_r, sem_w, sem_y_s, sem_y_r, sem_a_s, sem_a_r,
    sem_e_s, sem_e_r, sem_v_s, sem_v_r, sem_x_s,
):
    p = lax.axis_index("proto")
    y = lax.axis_index("crop")
    chip = p // 2
    core = p % 2
    width, protos = w_ref.shape
    w_raw = s_log.at[0:width]
    w_copy = pltpu.make_async_copy(w_ref, w_raw, sem_w.at[0])
    w_copy.start()
    crops = e_ref.shape[0]
    n_ct = crops // LANES
    n_pt = protos // LANES
    feat = width // (2 * n_chip)
    n_plane = 2 * n_chip
    n_z = 8
    n_x = n_chip // n_z
    chip_x = chip // n_z
    chip_z = chip % n_z
    groups = (0, 2, 1, 3)
    ahead = lax.rem(y + 1, n_y)
    across = lax.rem(y + 2, n_y)
    behind = lax.rem(y + n_y - 1, n_y)
    mine = protos // n_y
    sibling = p + 1 - 2 * core

    bar = pltpu.get_barrier_semaphore()

    def plane_peers(go):
        def step(i, c):
            go(lax.rem(p + i, n_plane))
            return c

        lax.fori_loop(24, n_plane, step, 0)
        lax.fori_loop(1, 24, step, 0)

    def greet(other):
        pl.semaphore_signal(bar, inc=1, device_id=(other, y), device_id_type=MESH)

    plane_peers(greet)
    for i in range(1, n_y):
        pl.semaphore_signal(bar, inc=1, device_id=(p, lax.rem(y + i, n_y)), device_id_type=MESH)

    for src, dst in ((t_ref, gt), (s_ref, gs)):
        for j in range(feat):
            for ct in range(n_ct):
                k = n_ct * j + ct
                dst[0, chip, core, k : k + 1, :] = src[j : j + 1, ct * LANES : (ct + 1) * LANES]

    def prep_w(i, c):
        cols = pl.ds(pl.multiple_of(i * 256, 256), 256)
        w = w_raw[:, cols]
        w = w * (1.0 / jnp.sqrt(jnp.sum(w * w, axis=0, keepdims=True) + EPS))
        hi, lo = split(w)
        w_cat[0:width, cols] = hi
        w_cat[width : 2 * width, cols] = hi
        w_cat[2 * width : 3 * width, cols] = lo
        return c

    pl.semaphore_wait(bar, n_plane - 1 + n_y - 1)

    def remote(src, dst, s, r, plane, crop):
        copy = pltpu.make_async_remote_copy(
            src_ref=src, dst_ref=dst, send_sem=s, recv_sem=r, device_id=(plane, crop), device_id_type=MESH
        )
        copy.start()
        return copy

    def gather_start(buf, k):
        for dx in groups[:2]:
            def go(dz, c):
                other = lax.rem(chip_x + dx, n_x) * n_z + lax.rem(chip_z + dz, n_z)
                here = buf.at[0, chip, core]
                remote(here, here, sem_g_s.at[k], sem_g_r.at[k, dx], other * 2 + core, y)
                return c

            lax.fori_loop(1 if dx == 0 else 0, n_z, go, 0)

    def slots_of(dx):
        return pl.ds(pl.multiple_of(lax.rem(chip_x + n_x - dx, n_x) * n_z, n_z), n_z)

    def gather_group(buf, k, dx):
        got = buf.at[0, pl.ds(0, n_z - 1 if dx == 0 else n_z), core]
        await_bytes(got, sem_g_r.at[k, dx])
        block = buf.at[0, slots_of(dx), core]
        if dx == 0:
            for far_x in (1, 3):
                over = lax.rem(chip_x + far_x, n_x) * n_z + chip_z
                remote(block, block, sem_x_s.at[k], sem_g_r.at[k, far_x], over * 2 + core, y)
        remote(block, block, sem_d_s.at[k], sem_d_r.at[k], sibling, y)

    def spread_group(buf, k, dx):
        block = buf.at[0, slots_of(dx), core]
        remote(block, buf.at[n_y - 1, slots_of(dx), core], sem_a_s.at[k, 0], sem_a_r.at[k, 0], p, ahead)
        remote(block, buf.at[1, slots_of(dx), core], sem_a_s.at[k, 1], sem_a_r.at[k, 1], p, behind)

    def gather_finish(buf, k):
        await_bytes(buf.at[0, :, core], sem_d_r.at[k])

    def share(buf, k, rel):
        block = buf.at[rel, :, core]
        remote(block, block, sem_e_s.at[k, rel - 1], sem_e_r.at[k, rel - 1], sibling, y)

    def near_finish(buf, k):
        await_bytes(buf.at[n_y - 1, :, core], sem_a_r.at[k, 0])
        await_bytes(buf.at[1, :, core], sem_a_r.at[k, 1])
        share(buf, k, 1)
        share(buf, k, 3)

    def relay(buf, k):
        low, high = pl.ds(0, n_chip // 2), pl.ds(n_chip // 2, n_chip // 2)
        remote(buf.at[3, low, core], buf.at[2, low, core], sem_a_s.at[k, 2], sem_a_r.at[k, 2], p, ahead)
        remote(buf.at[1, high, core], buf.at[2, high, core], sem_a_s.at[k, 3], sem_a_r.at[k, 3], p, behind)

    def far_finish(buf, k):
        for i in (2, 3):
            await_bytes(buf.at[2, pl.ds(0, n_chip // 2), core], sem_a_r.at[k, i])
        share(buf, k, 2)

    def unit(buf, rel, temp, cat, keep):
        flat[...] = buf[rel].reshape(flat.shape)
        for ct in range(n_ct):
            rows = pl.ds(ct * LANES, LANES)
            x = flat[pl.ds(ct, width, stride=n_ct), :]
            x = x * (1.0 / jnp.sqrt(jnp.sum(x * x, axis=0, keepdims=True) + EPS))
            if keep:
                hi, lo = split(x)
                base = rel * 3 * crops + ct * LANES
                z_cat[:, base : base + LANES] = hi
                z_cat[:, crops + base : crops + base + LANES] = lo
                z_cat[:, 2 * crops + base : 2 * crops + base + LANES] = hi
            xt = (x * (1.0 / temp)).T
            hi, lo = split(xt)
            cat[rows, 0:width] = hi
            cat[rows, width : 2 * width] = lo
            cat[rows, 2 * width : 3 * width] = hi

    def other_block(buf, k, rel, temp, dst, keep):
        await_bytes(buf.at[rel, :, core], sem_e_r.at[k, rel - 1])
        unit(buf, rel, temp, zt_cat, keep)
        cols = pl.ds(pl.multiple_of(y * mine, mine), mine)
        dst[rel - 1] = jnp.exp(nn(zt_cat[...], w_cat[:, cols]))

    def col_start(k):
        col_in[k, pl.ds(y, 1)] = col_out[k : k + 1]
        for i in range(1, n_y):
            pltpu.make_async_remote_copy(
                src_ref=col_out.at[k],
                dst_ref=col_in.at[k, y],
                send_sem=sem_c_s.at[k],
                recv_sem=sem_c_r.at[k],
                device_id=(p, lax.rem(y + i, n_y)),
                device_id_type=MESH,
            ).start()

    def col_finish(k):
        await_bytes(col_in.at[k, pl.ds(0, n_y - 1)], sem_c_r.at[k])
        total = col_in[k, 0]
        for i in range(1, n_y):
            total = total + col_in[k, i]
        ubuf[...] = 1.0 / total

    def row_start(k):
        row_in[k, pl.ds(p, 1)] = row_out[k : k + 1]

        def go(other):
            remote(row_out.at[k], row_in.at[k, p], sem_r_s.at[k], sem_r_r.at[k], other, y)

        plane_peers(go)

    def row_finish(k):
        await_bytes(row_in.at[k, pl.ds(0, n_plane - 1)], sem_r_r.at[k])
        return jnp.sum(row_in[k], axis=0)

    def to_rows(k):
        for ct in range(n_ct):
            block = tcol[ct * LANES : (ct + 1) * LANES, :].T
            row_out[k, ct : ct + 1, :] = jnp.sum(block, axis=0, keepdims=True)

    def to_column(values):
        for ct in range(n_ct):
            row = jnp.broadcast_to(values[ct : ct + 1, :], (LANES, LANES))
            vcol[ct * LANES : (ct + 1) * LANES, :] = row.T

    chunk = 64

    def lane_fold(x):
        total = x[:, 0:LANES]
        for j in range(1, n_pt):
            total = total + x[:, j * LANES : (j + 1) * LANES]
        return total

    def scaled_fold(rows):
        total = None
        for j in range(n_pt):
            x = e_ref[rows, j * LANES : (j + 1) * LANES]
            x = x * ubuf[j : j + 1, :]
            total = x if total is None else total + x
        return total

    def row_pass(k):
        def go(i, c):
            rows = pl.ds(pl.multiple_of(i * chunk, chunk), chunk)
            tcol[rows, :] = scaled_fold(rows)
            return c

        lax.fori_loop(0, crops // chunk, go, 0)
        to_rows(k)

    def col_pass(k):
        def go(i, acc):
            rows = pl.ds(pl.multiple_of(i * 32, 32), 32)
            v = vcol[rows, :]
            out = []
            for j in range(n_pt):
                x = e_ref[rows, j * LANES : (j + 1) * LANES] * v
                out.append(acc[j] + jnp.sum(x.reshape(4, 8, LANES), axis=0))
            return tuple(out)

        acc = lax.fori_loop(0, crops // 32, go, tuple(jnp.zeros((8, LANES), f32) for _ in range(n_pt)))
        for j in range(n_pt):
            col_out[k, j : j + 1, :] = jnp.sum(acc[j], axis=0, keepdims=True)

    gather_start(gt, 0)
    w_copy.wait()
    lax.fori_loop(0, protos // 256, prep_w, 0)
    for dx in groups:
        gather_group(gt, 0, dx)
        spread_group(gt, 0, dx)
    gather_start(gs, 1)
    gather_finish(gt, 0)
    unit(gt, 0, TEACHER_TEMP, zt_cat, False)

    wide = 1024

    def teacher_block(i, c):
        cols = pl.ds(pl.multiple_of(i * wide, wide), wide)
        e = jnp.exp(nn(zt_cat[...], w_cat[:, cols]))
        e_ref[:, cols] = e
        sums = jnp.sum(e, axis=0, keepdims=True)
        for j in range(wide // LANES):
            col_out[0, pl.ds(wide // LANES * i + j, 1), :] = sums[:, j * LANES : (j + 1) * LANES]
        return c

    lax.fori_loop(0, protos // wide, teacher_block, 0)
    col_start(0)
    near_finish(gt, 0)
    gather_group(gs, 1, 0)
    col_finish(0)
    row_pass(0)
    row_start(0)

    spread_group(gs, 1, 0)
    for dx in groups[1:]:
        gather_group(gs, 1, dx)
        if dx != groups[3]:
            spread_group(gs, 1, dx)
    gather_finish(gs, 1)
    unit(gs, 0, STUDENT_TEMP, zs_cat, True)

    def student_block(i, c):
        cols = pl.ds(pl.multiple_of(i * wide, wide), wide)
        s = nn(zs_cat[...], w_cat[:, cols])
        s_log[:, cols] = s
        es_ref[:, cols] = jnp.exp(s)
        return c

    lax.fori_loop(0, protos // wide, student_block, 0)
    def features_of(dst, scale_u):
        def go(r, c):
            rows = pl.ds(pl.multiple_of(r * 64, 64), 64)
            cross = None
            for j in range(n_pt):
                lanes = slice(j * LANES, (j + 1) * LANES)
                if scale_u:
                    g = e_ref[rows, lanes] * ubuf[j : j + 1, :]
                    term = g * s_log[rows, lanes]
                    cross = term if cross is None else cross + term
                else:
                    g = es_ref[rows, lanes]
                hi, lo = split(g)
                g_hi[rows, lanes] = hi
                g_lo[rows, lanes] = lo
            if scale_u:
                tcol[rows, :] = cross
            return c

        lax.fori_loop(0, crops // 64, go, 0)
        w_hi, w_lo = w_cat[0:width, :], w_cat[2 * width : 3 * width, :]
        dst[...] = nt(w_hi, g_hi[...]) + nt(w_hi, g_lo[...]) + nt(w_lo, g_hi[...])

    for k in (1, 2):
        to_column(1.0 / row_finish(k - 1))
        col_pass(k)
        col_start(k)
        if k == 1:
            def fold(i, c):
                rows = pl.ds(pl.multiple_of(i * chunk, chunk), chunk)
                tcol[rows, :] = lane_fold(es_ref[rows, :])
                return c

            lax.fori_loop(0, crops // chunk, fold, 0)
            to_rows(3)
            row_start(3)
            other_block(gt, 0, 1, TEACHER_TEMP, er, False)
        else:
            relay(gs, 1)
            far_finish(gt, 0)
            other_block(gs, 1, 1, STUDENT_TEMP, esr, True)
            other_block(gs, 1, 3, STUDENT_TEMP, esr, True)
        col_finish(k)
        row_pass(k)
        row_start(k)
        if k == 1:
            spread_group(gs, 1, groups[3])
            relay(gt, 0)
            other_block(gt, 0, 3, TEACHER_TEMP, er, False)
            features_of(a1, False)
            near_finish(gs, 1)
    features_of(a2, True)
    other_block(gt, 0, 2, TEACHER_TEMP, er, False)
    far_finish(gs, 1)
    last = row_finish(2)
    student_total = row_finish(3)
    far[0, 0:n_ct, :] = scale / last
    far[0, n_ct : 2 * n_ct, :] = scale / student_total
    for i in range(1, n_y):
        remote(far.at[0], far.at[n_y - i], sem_v_s.at[0], sem_v_r.at[0], p, lax.rem(y + i, n_y))

    def spread_columns(rel, v_dst, t_dst):
        for ct in range(n_ct):
            rows = slice(ct * LANES, (ct + 1) * LANES)
            for dst, k in ((v_dst, ct), (t_dst, n_ct + ct)):
                row = jnp.broadcast_to(far[rel, k : k + 1, :], (LANES, LANES))
                dst[rows, :] = row.T

    out_rows = width // n_y
    half = 256

    def rows_of(d):
        return pl.ds(pl.multiple_of(d * out_rows, 8), out_rows)

    def grads_of(rel, h):
        def go(r, c):
            rows = pl.ds(pl.multiple_of(r * 64, 64), 64)
            v = vfar[rel, rows, :]
            t = tfar[rel, rows, :]
            for j in range(h * half // LANES, (h + 1) * half // LANES):
                u = ubuf[pl.ds(y * (mine // LANES) + j, 1), :]
                lanes = slice(j * LANES, (j + 1) * LANES)
                if rel == 0:
                    here = pl.ds(pl.multiple_of(y * mine + j * LANES, LANES), LANES)
                    e, es = e_ref[rows, here], es_ref[rows, here]
                else:
                    e, es = er[rel - 1, rows, lanes], esr[rel - 1, rows, lanes]
                hi, lo = split(es * t - e * u * v)
                base = pl.multiple_of(rel * 3 * crops + r * 64, 64)
                g_cat[pl.ds(base, 64), lanes] = hi
                g_cat[pl.ds(base + crops, 64), lanes] = hi
                g_cat[pl.ds(base + 2 * crops, 64), lanes] = lo
            return c

        lax.fori_loop(0, crops // 64, go, 0)

    def proto_part(h):
        part[h] = jnp.zeros((width, half), f32)

        def go(q, c):
            k = pl.ds(pl.multiple_of(q * 3 * crops, 3 * crops), 3 * crops)
            part[h] += nn(z_cat[:, k], g_cat[k, h * half : (h + 1) * half])
            return c

        lax.fori_loop(0, n_y, go, 0)
        final[h, pl.ds(y, 1)] = part[h, rows_of(y)][None]
        for i in (2, 1, 3):
            to = lax.rem(y + i, n_y)
            remote(part.at[h, rows_of(to)], final.at[h, y], sem_y_s.at[h], sem_y_r.at[h], p, to)

    spread_columns(0, vfar.at[0], tfar.at[0])

    cross = jnp.sum(tcol[...] * vfar[0], axis=0, keepdims=True)
    lse = jnp.sum(jnp.log(student_total), axis=0, keepdims=True)
    for ct in range(n_ct):
        lanes = slice(ct * LANES, (ct + 1) * LANES)
        t, v = far[0, n_ct + ct : n_ct + ct + 1, :], far[0, ct : ct + 1, :]
        rs_flat[pl.ds(ct, width, stride=n_ct), :] = a1[:, lanes] * t - a2[:, lanes] * v
    slab = feat * n_ct
    rs_src[:, :, 0:slab, :] = rs_flat[...].reshape((n_chip, 2, slab, LANES))
    loss_row = lse * (1.0 / n_plane) - cross * (1.0 / scale)
    rs_src[:, :, slab : slab + 1, :] = jnp.broadcast_to(loss_row, (n_chip, 2, 1, LANES))
    pair = pltpu.make_async_remote_copy(
        src_ref=rs_src.at[:, 1 - core],
        dst_ref=rs_pair,
        send_sem=sem_f_s.at[0],
        recv_sem=sem_f_r.at[0],
        device_id=(p + 1 - 2 * core, y),
        device_id_type=MESH,
    )
    pair.start()
    for h in range(mine // 256):
        grads_of(0, h)
    other_block(gs, 1, 2, STUDENT_TEMP, esr, True)
    pair.wait()
    rs_pair[...] += rs_src[:, core]
    rs_in[pl.ds(chip, 1)] = rs_pair[pl.ds(chip, 1)]

    def scatter(i, c):
        other = lax.rem(chip + i, n_chip)
        pltpu.make_async_remote_copy(
            src_ref=rs_pair.at[other],
            dst_ref=rs_in.at[chip],
            send_sem=sem_f_s.at[1],
            recv_sem=sem_f_r.at[1],
            device_id=(other * 2 + core, y),
            device_id_type=MESH,
        ).start()
        return c

    lax.fori_loop(1, n_chip, scatter, 0)
    await_bytes(far.at[pl.ds(1, n_y - 1)], sem_v_r.at[0])
    for rel in range(1, n_y):
        spread_columns(rel, vfar.at[rel], tfar.at[rel])
    for h in range(mine // half):
        for rel in range(1, n_y):
            grads_of(rel, h)
        proto_part(h)

    await_bytes(rs_in.at[pl.ds(0, n_chip - 1)], sem_f_r.at[1])
    total = jnp.sum(rs_in[...], axis=0)
    loss_in[pl.ds(y, 1)] = total[slab : slab + 1, :][None]
    for i in range(1, n_y):
        remote(loss_in.at[y], loss_in.at[y], sem_l_s.at[0], sem_l_r.at[0], p, lax.rem(y + i, n_y))
    for j in range(feat):
        for ct in range(n_ct):
            k = n_ct * j + ct
            gf_ref[j : j + 1, ct * LANES : (ct + 1) * LANES] = total[k : k + 1, :]
    for h in range(mine // half):
        await_bytes(final.at[h, pl.ds(0, n_y - 1)], sem_y_r.at[h])
        for q in range(n_y):
            gp_ref[:, q * mine + h * half : q * mine + (h + 1) * half] = final[h, q]
    await_bytes(loss_in.at[pl.ds(0, n_y - 1)], sem_l_r.at[0])
    loss_ref[0, 0] = jnp.sum(jnp.sum(loss_in[...], axis=0)) * (1.0 / crops_all)

    for k, buf in ((0, gt), (1, gs)):
        await_bytes(buf.at[0, pl.ds(0, 2 * n_z - 1), core], sem_g_s.at[k])
        await_bytes(buf.at[0, pl.ds(0, 2 * n_z), core], sem_x_s.at[k])
        await_bytes(buf.at[0, :, core], sem_d_s.at[k])
        for i in range(2):
            await_bytes(buf.at[0, :, core], sem_a_s.at[k, i])
            await_bytes(buf.at[0, pl.ds(0, n_chip // 2), core], sem_a_s.at[k, 2 + i])
        for i in range(n_y - 1):
            await_bytes(buf.at[0, :, core], sem_e_s.at[k, i])
    await_bytes(far.at[pl.ds(1, n_y - 1)], sem_v_s.at[0])
    for h in range(mine // half):
        await_bytes(final.at[h, pl.ds(0, n_y - 1)], sem_y_s.at[h])
    await_bytes(loss_in.at[pl.ds(0, n_y - 1)], sem_l_s.at[0])
    await_bytes(rs_in.at[pl.ds(0, n_chip - 1)], sem_f_s.at[1])
    for k in range(3):
        await_bytes(col_in.at[k, pl.ds(0, n_y - 1)], sem_c_s.at[k])
    for k in range(4):
        await_bytes(row_in.at[k, pl.ds(0, n_plane - 1)], sem_r_s.at[k])


def on_device(n_y, n_chip, t, s, w):
    width, protos = w.shape
    feat, crops = t.shape
    n_ct = crops // LANES
    n_pt = protos // LANES
    n_plane = 2 * n_chip
    scale = math.sqrt(protos * n_plane) / STUDENT_TEMP
    vm = pltpu.VMEM
    dma = pltpu.SemaphoreType.DMA
    slots = (n_chip, 2, feat * n_ct, LANES)
    mine = protos // n_y
    gf, gp, loss = pl.pallas_call(
        functools.partial(kernel, n_y, n_chip, scale, crops * n_y),
        out_shape=(
            jax.ShapeDtypeStruct((feat, crops), f32),
            jax.ShapeDtypeStruct((width // n_y, protos), f32),
            jax.ShapeDtypeStruct((1, 1), f32),
        ),
        in_specs=[
            pl.BlockSpec(memory_space=vm),
            pl.BlockSpec(memory_space=vm),
            pl.BlockSpec(memory_space=pl.ANY),
        ],
        out_specs=(
            pl.BlockSpec(memory_space=vm),
            pl.BlockSpec(memory_space=vm),
            pl.BlockSpec(memory_space=pltpu.SMEM),
        ),
        scratch_shapes=[
            vm((n_y,) + slots, f32),
            vm((n_y,) + slots, f32),
            vm((width * n_ct, LANES), f32),
            vm((crops, 3 * width), bf16),
            vm((crops, 3 * width), bf16),
            vm((width, 3 * n_y * crops), bf16),
            vm((3 * width, protos), bf16),
            vm((crops, protos), f32),
            vm((crops, protos), f32),
            vm((crops, protos), f32),
            vm((crops, protos), bf16),
            vm((crops, protos), bf16),
            vm((n_y - 1, crops, mine), f32),
            vm((n_y - 1, crops, mine), f32),
            vm((3 * n_y * crops, mine), bf16),
            vm((n_y, 2 * n_ct, LANES), f32),
            vm((n_y, crops, LANES), f32),
            vm((n_y, crops, LANES), f32),
            vm((width, crops), f32),
            vm((width, crops), f32),
            vm((crops, LANES), f32),
            vm((crops, LANES), f32),
            vm((3, n_pt, LANES), f32),
            vm((3, n_y, n_pt, LANES), f32),
            vm((n_pt, LANES), f32),
            vm((4, n_ct, LANES), f32),
            vm((4, n_plane, n_ct, LANES), f32),
            vm((width * n_ct, LANES), f32),
            vm((n_chip, 2, feat * n_ct + 1, LANES), f32),
            vm((n_chip, feat * n_ct + 1, LANES), f32),
            vm((n_chip, feat * n_ct + 1, LANES), f32),
            vm((n_y, 1, LANES), f32),
            vm((mine // 256, width, 256), f32),
            vm((mine // 256, n_y, width // n_y, 256), f32),
            dma((2,)), dma((2, 4)), dma((2,)), dma((2,)), dma((3,)), dma((3,)), dma((4,)), dma((4,)),
            dma((2,)), dma((2,)), dma((1,)), dma((1,)),
            dma((1,)), dma((mine // 256,)), dma((mine // 256,)), dma((2, 4)), dma((2, 4)),
            dma((2, 3)), dma((2, 3)), dma((1,)), dma((1,)), dma((2,)),
        ],
        compiler_params=pltpu.CompilerParams(
            collective_id=0, has_side_effects=True, vmem_limit_bytes=60 * 2**20
        ),
    )(t, s, w)
    return gf, gp, loss.reshape(())


def solution(mesh):
    placed = (P("proto", "crop"), P("proto", "crop"), P(None, "proto"))
    n_y = mesh.shape["crop"]
    n_chip = mesh.shape["proto"] // 2
    return jax.shard_map(
        functools.partial(on_device, n_y, n_chip),
        mesh=mesh,
        in_specs=placed,
        out_specs=(P("proto", "crop"), P("crop", "proto"), P()),
        check_vma=False,
    )
```

```python
import functools
import math

import jax
import jax.numpy as jnp
from jax import lax
from jax.experimental import pallas as pl
from jax.experimental.pallas import tpu as pltpu
from jax.sharding import PartitionSpec as P

MESH = pl.DeviceIdType.MESH
TEACHER_TEMP = 0.07
STUDENT_TEMP = 0.1
EPS = 1e-06
ITERS = 3
f32 = jnp.float32
bf16 = jnp.bfloat16
LANES = 128


def split(x):
    hi = x.astype(bf16)
    return hi, (x - hi.astype(f32)).astype(bf16)


def await_bytes(ref, sem):
    pltpu.make_async_copy(ref, ref, sem).wait()


def nn(a, b):
    return lax.dot_general(a, b, (((1,), (0,)), ((), ())), preferred_element_type=f32)


def nt(a, b):
    return lax.dot_general(a, b, (((1,), (1,)), ((), ())), preferred_element_type=f32)


def kernel(
    n_y, n_chip, scale, crops_all,
    t_ref, s_ref, w_ref,
    gf_ref, gp_ref, loss_ref,
    gt, gs, flat, zt_cat, zs_cat, z_cat, w_cat, e_ref, s_log, es_ref, g_hi, g_lo,
    er, esr, g_cat, far, vfar, tfar, a1, a2,
    tcol, vcol, col_out, col_in, ubuf, row_out, row_in, rs_flat, rs_src, rs_pair, rs_in,
    loss_in, loss_sum, part, final, t_raw, s_raw,
    sem_g_s, sem_g_r, sem_d_s, sem_d_r, sem_c_s, sem_c_r, sem_r_s, sem_r_r, sem_f_s, sem_f_r,
    sem_l_s, sem_l_r, sem_w, sem_y_s, sem_y_r, sem_a_s, sem_a_r,
    sem_e_s, sem_e_r, sem_v_s, sem_v_r, sem_x_s,
):
    p = lax.axis_index("proto")
    y = lax.axis_index("crop")
    chip = p // 2
    core = p % 2
    width, protos = w_ref.shape
    w_raw = s_log.at[0:width]
    t_copy = pltpu.make_async_copy(t_ref, t_raw, sem_w.at[1])
    s_copy = pltpu.make_async_copy(s_ref, s_raw, sem_w.at[2])
    w_copy = pltpu.make_async_copy(w_ref, w_raw, sem_w.at[0])
    t_copy.start()
    s_copy.start()
    w_copy.start()
    crops = e_ref.shape[0]
    n_ct = crops // LANES
    n_pt = protos // LANES
    feat = width // (2 * n_chip)
    n_plane = 2 * n_chip
    n_z = 8
    n_x = n_chip // n_z
    chip_x = chip // n_z
    chip_z = chip % n_z
    groups = (0, 2, 1, 3)
    ahead = lax.rem(y + 1, n_y)
    across = lax.rem(y + 2, n_y)
    behind = lax.rem(y + n_y - 1, n_y)
    mine = protos // n_y
    sibling = p + 1 - 2 * core

    bar = pltpu.get_barrier_semaphore()

    def plane_peers(go):
        def step(i, c):
            go(lax.rem(p + i, n_plane))
            return c

        lax.fori_loop(24, n_plane, step, 0)
        lax.fori_loop(1, 24, step, 0)

    def greet(other):
        pl.semaphore_signal(bar, inc=1, device_id=(other, y), device_id_type=MESH)

    plane_peers(greet)
    for i in range(1, n_y):
        for to in (p, sibling):
            pl.semaphore_signal(bar, inc=1, device_id=(to, lax.rem(y + i, n_y)), device_id_type=MESH)

    t_copy.wait()
    s_copy.wait()
    for src, dst in ((t_raw, gt), (s_raw, gs)):
        for j in range(feat):
            for ct in range(n_ct):
                k = n_ct * j + ct
                dst[0, chip, core, k : k + 1, :] = src[j : j + 1, ct * LANES : (ct + 1) * LANES]

    def prep_w(i, c):
        cols = pl.ds(pl.multiple_of(i * 256, 256), 256)
        w = w_raw[:, cols]
        w = w * (1.0 / jnp.sqrt(jnp.sum(w * w, axis=0, keepdims=True) + EPS))
        hi, lo = split(w)
        w_cat[0:width, cols] = hi
        w_cat[width : 2 * width, cols] = hi
        w_cat[2 * width : 3 * width, cols] = lo
        return c

    pl.semaphore_wait(bar, n_plane - 1 + 2 * (n_y - 1))

    def remote(src, dst, s, r, plane, crop):
        copy = pltpu.make_async_remote_copy(
            src_ref=src, dst_ref=dst, send_sem=s, recv_sem=r, device_id=(plane, crop), device_id_type=MESH
        )
        copy.start()
        return copy

    def gather_start(buf, k):
        for dx in groups[:2]:
            def go(dz, c):
                other = lax.rem(chip_x + dx, n_x) * n_z + lax.rem(chip_z + dz, n_z)
                here = buf.at[0, chip, core]
                remote(here, here, sem_g_s.at[k], sem_g_r.at[k, dx], other * 2 + core, y)
                return c

            lax.fori_loop(1 if dx == 0 else 0, n_z, go, 0)

    def slots_of(dx):
        return pl.ds(pl.multiple_of(lax.rem(chip_x + n_x - dx, n_x) * n_z, n_z), n_z)

    def gather_group(buf, k, dx):
        got = buf.at[0, pl.ds(0, n_z - 1 if dx == 0 else n_z), core]
        await_bytes(got, sem_g_r.at[k, dx])
        block = buf.at[0, slots_of(dx), core]
        if dx == 0:
            for far_x in (1, 3):
                over = lax.rem(chip_x + far_x, n_x) * n_z + chip_z
                remote(block, block, sem_x_s.at[k], sem_g_r.at[k, far_x], over * 2 + core, y)
        remote(block, block, sem_d_s.at[k], sem_d_r.at[k], sibling, y)

    def spread_group(buf, k, dx):
        block = buf.at[0, slots_of(dx), core]
        remote(block, buf.at[n_y - 1, slots_of(dx), core], sem_a_s.at[k, 0], sem_a_r.at[k, 0], p, ahead)
        remote(block, buf.at[1, slots_of(dx), core], sem_a_s.at[k, 1], sem_a_r.at[k, 1], p, behind)

    def gather_finish(buf, k):
        await_bytes(buf.at[0, :, core], sem_d_r.at[k])

    def share(buf, k, rel):
        block = buf.at[rel, :, core]
        remote(block, block, sem_e_s.at[k, rel - 1], sem_e_r.at[k, rel - 1], sibling, y)

    def near_finish(buf, k):
        await_bytes(buf.at[n_y - 1, :, core], sem_a_r.at[k, 0])
        await_bytes(buf.at[1, :, core], sem_a_r.at[k, 1])
        share(buf, k, 1)
        share(buf, k, 3)

    def relay(buf, k):
        low, high = pl.ds(0, n_chip // 2), pl.ds(n_chip // 2, n_chip // 2)
        remote(buf.at[3, low, core], buf.at[2, low, core], sem_a_s.at[k, 2], sem_a_r.at[k, 2], p, ahead)
        remote(buf.at[1, high, core], buf.at[2, high, core], sem_a_s.at[k, 3], sem_a_r.at[k, 3], p, behind)

    def far_finish(buf, k):
        for i in (2, 3):
            await_bytes(buf.at[2, pl.ds(0, n_chip // 2), core], sem_a_r.at[k, i])
        share(buf, k, 2)

    def unit(buf, rel, temp, cat, keep):
        flat[...] = buf[rel].reshape(flat.shape)
        for ct in range(n_ct):
            rows = pl.ds(ct * LANES, LANES)
            x = flat[pl.ds(ct, width, stride=n_ct), :]
            x = x * (1.0 / jnp.sqrt(jnp.sum(x * x, axis=0, keepdims=True) + EPS))
            if keep:
                hi, lo = split(x)
                base = rel * 3 * crops + ct * LANES
                z_cat[:, base : base + LANES] = hi
                z_cat[:, crops + base : crops + base + LANES] = lo
                z_cat[:, 2 * crops + base : 2 * crops + base + LANES] = hi
            xt = (x * (1.0 / temp)).T
            hi, lo = split(xt)
            cat[rows, 0:width] = hi
            cat[rows, width : 2 * width] = lo
            cat[rows, 2 * width : 3 * width] = hi

    def other_block(buf, k, rel, temp, dst, keep):
        await_bytes(buf.at[rel, :, core], sem_e_r.at[k, rel - 1])
        unit(buf, rel, temp, zt_cat, keep)
        cols = pl.ds(pl.multiple_of(y * mine, mine), mine)
        dst[rel - 1] = jnp.exp(nn(zt_cat[...], w_cat[:, cols]))

    def col_start(k):
        col_in[k, pl.ds(y, 1)] = col_out[k : k + 1]
        for i in range(1, n_y):
            pltpu.make_async_remote_copy(
                src_ref=col_out.at[k],
                dst_ref=col_in.at[k, y],
                send_sem=sem_c_s.at[k],
                recv_sem=sem_c_r.at[k],
                device_id=(p, lax.rem(y + i, n_y)),
                device_id_type=MESH,
            ).start()

    def col_finish(k):
        await_bytes(col_in.at[k, pl.ds(0, n_y - 1)], sem_c_r.at[k])
        total = col_in[k, 0]
        for i in range(1, n_y):
            total = total + col_in[k, i]
        ubuf[...] = 1.0 / total

    def row_start(k):
        row_in[k, pl.ds(p, 1)] = row_out[k : k + 1]

        def go(other):
            remote(row_out.at[k], row_in.at[k, p], sem_r_s.at[k], sem_r_r.at[k], other, y)

        plane_peers(go)

    def row_finish(k):
        await_bytes(row_in.at[k, pl.ds(0, n_plane - 1)], sem_r_r.at[k])
        return jnp.sum(row_in[k], axis=0)

    def to_rows(k):
        for ct in range(n_ct):
            block = tcol[ct * LANES : (ct + 1) * LANES, :].T
            row_out[k, ct : ct + 1, :] = jnp.sum(block, axis=0, keepdims=True)

    def to_column(values):
        for ct in range(n_ct):
            row = jnp.broadcast_to(values[ct : ct + 1, :], (LANES, LANES))
            vcol[ct * LANES : (ct + 1) * LANES, :] = row.T

    chunk = 64

    def lane_fold(x):
        total = x[:, 0:LANES]
        for j in range(1, n_pt):
            total = total + x[:, j * LANES : (j + 1) * LANES]
        return total

    def scaled_fold(rows):
        total = None
        for j in range(n_pt):
            x = e_ref[rows, j * LANES : (j + 1) * LANES]
            x = x * ubuf[j : j + 1, :]
            total = x if total is None else total + x
        return total

    def row_pass(k):
        def go(i, c):
            rows = pl.ds(pl.multiple_of(i * chunk, chunk), chunk)
            tcol[rows, :] = scaled_fold(rows)
            return c

        lax.fori_loop(0, crops // chunk, go, 0)
        to_rows(k)

    def col_pass(k):
        def go(i, acc):
            rows = pl.ds(pl.multiple_of(i * 32, 32), 32)
            v = vcol[rows, :]
            out = []
            for j in range(n_pt):
                x = e_ref[rows, j * LANES : (j + 1) * LANES] * v
                out.append(acc[j] + jnp.sum(x.reshape(4, 8, LANES), axis=0))
            return tuple(out)

        acc = lax.fori_loop(0, crops // 32, go, tuple(jnp.zeros((8, LANES), f32) for _ in range(n_pt)))
        for j in range(n_pt):
            col_out[k, j : j + 1, :] = jnp.sum(acc[j], axis=0, keepdims=True)

    gather_start(gt, 0)
    w_copy.wait()
    lax.fori_loop(0, protos // 256, prep_w, 0)
    for dx in groups:
        gather_group(gt, 0, dx)
        spread_group(gt, 0, dx)
    gather_start(gs, 1)
    gather_finish(gt, 0)
    unit(gt, 0, TEACHER_TEMP, zt_cat, False)

    wide = 1024

    def teacher_block(i, c):
        cols = pl.ds(pl.multiple_of(i * wide, wide), wide)
        e = jnp.exp(nn(zt_cat[...], w_cat[:, cols]))
        e_ref[:, cols] = e
        sums = jnp.sum(e, axis=0, keepdims=True)
        for j in range(wide // LANES):
            col_out[0, pl.ds(wide // LANES * i + j, 1), :] = sums[:, j * LANES : (j + 1) * LANES]
        return c

    lax.fori_loop(0, protos // wide, teacher_block, 0)
    col_start(0)
    gather_group(gs, 1, 0)
    near_finish(gt, 0)
    col_finish(0)
    row_pass(0)
    row_start(0)
    spread_group(gs, 1, 0)
    for dx in groups[1:]:
        gather_group(gs, 1, dx)
        if dx != groups[3]:
            spread_group(gs, 1, dx)
    gather_finish(gs, 1)
    unit(gs, 0, STUDENT_TEMP, zs_cat, True)

    def student_block(i, c):
        cols = pl.ds(pl.multiple_of(i * wide, wide), wide)
        s = nn(zs_cat[...], w_cat[:, cols])
        s_log[:, cols] = s
        es_ref[:, cols] = jnp.exp(s)
        return c

    lax.fori_loop(0, protos // wide, student_block, 0)
    def features_of(dst, scale_u):
        def go(r, c):
            rows = pl.ds(pl.multiple_of(r * 64, 64), 64)
            cross = None
            for j in range(n_pt):
                lanes = slice(j * LANES, (j + 1) * LANES)
                if scale_u:
                    g = e_ref[rows, lanes] * ubuf[j : j + 1, :]
                    term = g * s_log[rows, lanes]
                    cross = term if cross is None else cross + term
                else:
                    g = es_ref[rows, lanes]
                hi, lo = split(g)
                g_hi[rows, lanes] = hi
                g_lo[rows, lanes] = lo
            if scale_u:
                tcol[rows, :] = cross
            return c

        lax.fori_loop(0, crops // 64, go, 0)
        w_hi, w_lo = w_cat[0:width, :], w_cat[2 * width : 3 * width, :]
        dst[...] = nt(w_hi, g_hi[...]) + nt(w_hi, g_lo[...]) + nt(w_lo, g_hi[...])

    for k in (1, 2):
        to_column(1.0 / row_finish(k - 1))
        col_pass(k)
        col_start(k)
        if k == 1:
            relay(gt, 0)

            def fold(i, c):
                rows = pl.ds(pl.multiple_of(i * chunk, chunk), chunk)
                tcol[rows, :] = lane_fold(es_ref[rows, :])
                return c

            lax.fori_loop(0, crops // chunk, fold, 0)
            to_rows(3)
            row_start(3)
            other_block(gt, 0, 1, TEACHER_TEMP, er, False)
        else:
            relay(gs, 1)
            other_block(gt, 0, 2, TEACHER_TEMP, er, False)
            other_block(gs, 1, 1, STUDENT_TEMP, esr, True)
        col_finish(k)
        row_pass(k)
        row_start(k)
        if k == 1:
            spread_group(gs, 1, groups[3])
            other_block(gt, 0, 3, TEACHER_TEMP, er, False)
            features_of(a1, False)
            far_finish(gt, 0)
            near_finish(gs, 1)
    features_of(a2, True)
    other_block(gs, 1, 3, STUDENT_TEMP, esr, True)
    far_finish(gs, 1)
    last = row_finish(2)
    student_total = row_finish(3)
    far[0, 0:n_ct, :] = scale / last
    far[0, n_ct : 2 * n_ct, :] = scale / student_total
    for i in range(1, n_y):
        remote(far.at[0], far.at[n_y - i], sem_v_s.at[0], sem_v_r.at[0], p, lax.rem(y + i, n_y))

    def spread_columns(rel, v_dst, t_dst):
        for ct in range(n_ct):
            rows = slice(ct * LANES, (ct + 1) * LANES)
            for dst, k in ((v_dst, ct), (t_dst, n_ct + ct)):
                row = jnp.broadcast_to(far[rel, k : k + 1, :], (LANES, LANES))
                dst[rows, :] = row.T

    out_rows = width // n_y
    half = LANES

    def rows_of(d):
        return pl.ds(pl.multiple_of(d * out_rows, 8), out_rows)

    def grads_of(rel, c0):
        lanes = pl.ds(pl.multiple_of(c0 * LANES, LANES), LANES)
        here = pl.ds(pl.multiple_of(y * mine + c0 * LANES, LANES), LANES)
        u = ubuf[pl.ds(y * (mine // LANES) + c0, 1), :]

        def go(r, c):
            rows = pl.ds(pl.multiple_of(r * 64, 64), 64)
            v = vfar[rel, rows, :]
            t = tfar[rel, rows, :]
            if rel == 0:
                e, es = e_ref[rows, here], es_ref[rows, here]
            else:
                e, es = er[rel - 1, rows, lanes], esr[rel - 1, rows, lanes]
            hi, lo = split(es * t - e * u * v)
            base = pl.multiple_of(rel * 3 * crops + r * 64, 64)
            g_cat[pl.ds(base, 64), lanes] = hi
            g_cat[pl.ds(base + crops, 64), lanes] = hi
            g_cat[pl.ds(base + 2 * crops, 64), lanes] = lo
            return c

        lax.fori_loop(0, crops // 64, go, 0)

    def proto_part(h, carry):
        for rel in range(1, n_y):
            grads_of(rel, h)
        lanes = pl.ds(pl.multiple_of(h * half, half), half)
        part[h] = nn(z_cat[...], g_cat[:, lanes])
        final[h, pl.ds(y, 1)] = part[h, rows_of(y)][None]
        for i in (2, 1, 3):
            to = lax.rem(y + i, n_y)
            remote(part.at[h, rows_of(to)], final.at[h, y], sem_y_s.at[h], sem_y_r.at[h], p, to)
        return carry

    spread_columns(0, vfar.at[0], tfar.at[0])

    cross = jnp.sum(tcol[...] * vfar[0], axis=0, keepdims=True)
    lse = jnp.sum(jnp.log(student_total), axis=0, keepdims=True)
    loss_in[pl.ds(2 * y + core, 1)] = (lse * (1.0 / n_plane) - cross * (1.0 / scale))[None]
    for i in range(n_y):
        for c in range(2):
            if i or c:
                here = loss_in.at[2 * y + core]
                to = 2 * chip + lax.rem(core + c, 2)
                remote(here, here, sem_l_s.at[0], sem_l_r.at[0], to, lax.rem(y + i, n_y))
    for ct in range(n_ct):
        lanes = slice(ct * LANES, (ct + 1) * LANES)
        t, v = far[0, n_ct + ct : n_ct + ct + 1, :], far[0, ct : ct + 1, :]
        rs_flat[pl.ds(ct, width, stride=n_ct), :] = a1[:, lanes] * t - a2[:, lanes] * v
    rs_src[...] = rs_flat[...].reshape(rs_src.shape)
    pair = pltpu.make_async_remote_copy(
        src_ref=rs_src.at[:, 1 - core],
        dst_ref=rs_pair,
        send_sem=sem_f_s.at[0],
        recv_sem=sem_f_r.at[0],
        device_id=(p + 1 - 2 * core, y),
        device_id_type=MESH,
    )
    pair.start()
    lax.fori_loop(0, mine // half, lambda h, c: (grads_of(0, h), c)[1], 0)
    pair.wait()
    rs_pair[...] += rs_src[:, core]
    rs_in[pl.ds(chip, 1)] = rs_pair[pl.ds(chip, 1)]

    def scatter(i, c):
        other = lax.rem(chip + i, n_chip)
        pltpu.make_async_remote_copy(
            src_ref=rs_pair.at[other],
            dst_ref=rs_in.at[chip],
            send_sem=sem_f_s.at[1],
            recv_sem=sem_f_r.at[1],
            device_id=(other * 2 + core, y),
            device_id_type=MESH,
        ).start()
        return c

    lax.fori_loop(1, n_chip, scatter, 0)
    other_block(gs, 1, 2, STUDENT_TEMP, esr, True)
    await_bytes(far.at[pl.ds(1, n_y - 1)], sem_v_r.at[0])
    for rel in range(1, n_y):
        spread_columns(rel, vfar.at[rel], tfar.at[rel])
    lax.fori_loop(0, mine // half, proto_part, 0)
    await_bytes(loss_in.at[pl.ds(0, 2 * n_y - 1)], sem_l_r.at[0])
    loss_sum[pl.ds(chip, 1)] = jnp.sum(loss_in[...], axis=0, keepdims=True)

    def scatter_loss(i, c):
        here = loss_sum.at[chip]
        remote(here, here, sem_l_s.at[1], sem_l_r.at[1], lax.rem(chip + i, n_chip) * 2 + core, y)
        return c

    lax.fori_loop(1, n_chip, scatter_loss, 0)

    await_bytes(rs_in.at[pl.ds(0, n_chip - 1)], sem_f_r.at[1])
    total = jnp.sum(rs_in[...], axis=0)
    for j in range(feat):
        for ct in range(n_ct):
            k = n_ct * j + ct
            gf_ref[j : j + 1, ct * LANES : (ct + 1) * LANES] = total[k : k + 1, :]
    for h in range(mine // half):
        await_bytes(final.at[h, pl.ds(0, n_y - 1)], sem_y_r.at[h])
        for q in range(n_y):
            gp_ref[:, q * mine + h * half : q * mine + (h + 1) * half] = final[h, q]
    await_bytes(loss_sum.at[pl.ds(0, n_chip - 1)], sem_l_r.at[1])
    loss_ref[0, 0] = jnp.sum(jnp.sum(loss_sum[...], axis=0)) * (1.0 / crops_all)

    for k, buf in ((0, gt), (1, gs)):
        await_bytes(buf.at[0, pl.ds(0, 2 * n_z - 1), core], sem_g_s.at[k])
        await_bytes(buf.at[0, pl.ds(0, 2 * n_z), core], sem_x_s.at[k])
        await_bytes(buf.at[0, :, core], sem_d_s.at[k])
        for i in range(2):
            await_bytes(buf.at[0, :, core], sem_a_s.at[k, i])
            await_bytes(buf.at[0, pl.ds(0, n_chip // 2), core], sem_a_s.at[k, 2 + i])
        for i in range(n_y - 1):
            await_bytes(buf.at[0, :, core], sem_e_s.at[k, i])
    await_bytes(far.at[pl.ds(1, n_y - 1)], sem_v_s.at[0])
    for h in range(mine // half):
        await_bytes(final.at[h, pl.ds(0, n_y - 1)], sem_y_s.at[h])
    await_bytes(loss_in.at[pl.ds(0, 2 * n_y - 1)], sem_l_s.at[0])
    await_bytes(loss_sum.at[pl.ds(0, n_chip - 1)], sem_l_s.at[1])
    await_bytes(rs_in.at[pl.ds(0, n_chip - 1)], sem_f_s.at[1])
    for k in range(3):
        await_bytes(col_in.at[k, pl.ds(0, n_y - 1)], sem_c_s.at[k])
    for k in range(4):
        await_bytes(row_in.at[k, pl.ds(0, n_plane - 1)], sem_r_s.at[k])


def on_device(n_y, n_chip, t, s, w):
    width, protos = w.shape
    feat, crops = t.shape
    n_ct = crops // LANES
    n_pt = protos // LANES
    n_plane = 2 * n_chip
    scale = math.sqrt(protos * n_plane) / STUDENT_TEMP
    vm = pltpu.VMEM
    dma = pltpu.SemaphoreType.DMA
    slots = (n_chip, 2, feat * n_ct, LANES)
    mine = protos // n_y
    gf, gp, loss = pl.pallas_call(
        functools.partial(kernel, n_y, n_chip, scale, crops * n_y),
        out_shape=(
            pltpu.VMEM((feat, crops), f32),
            pltpu.VMEM((width // n_y, protos), f32),
            jax.ShapeDtypeStruct((1, 1), f32),
        ),
        in_specs=[
            pl.BlockSpec(memory_space=pl.ANY),
            pl.BlockSpec(memory_space=pl.ANY),
            pl.BlockSpec(memory_space=pl.ANY),
        ],
        out_specs=(
            pl.BlockSpec(memory_space=vm),
            pl.BlockSpec(memory_space=vm),
            pl.BlockSpec(memory_space=pltpu.SMEM),
        ),
        scratch_shapes=[
            vm((n_y,) + slots, f32),
            vm((n_y,) + slots, f32),
            vm((width * n_ct, LANES), f32),
            vm((crops, 3 * width), bf16),
            vm((crops, 3 * width), bf16),
            vm((width, 3 * n_y * crops), bf16),
            vm((3 * width, protos), bf16),
            vm((crops, protos), f32),
            vm((crops, protos), f32),
            vm((crops, protos), f32),
            vm((crops, protos), bf16),
            vm((crops, protos), bf16),
            vm((n_y - 1, crops, mine), f32),
            vm((n_y - 1, crops, mine), f32),
            vm((3 * n_y * crops, mine), bf16),
            vm((n_y, 2 * n_ct, LANES), f32),
            vm((n_y, crops, LANES), f32),
            vm((n_y, crops, LANES), f32),
            vm((width, crops), f32),
            vm((width, crops), f32),
            vm((crops, LANES), f32),
            vm((crops, LANES), f32),
            vm((3, n_pt, LANES), f32),
            vm((3, n_y, n_pt, LANES), f32),
            vm((n_pt, LANES), f32),
            vm((4, n_ct, LANES), f32),
            vm((4, n_plane, n_ct, LANES), f32),
            vm((width * n_ct, LANES), f32),
            vm(slots, f32),
            vm(slots[:1] + slots[2:], f32),
            vm(slots[:1] + slots[2:], f32),
            vm((2 * n_y, 1, LANES), f32),
            vm((n_chip, 1, LANES), f32),
            vm((mine // 128, width, 128), f32),
            vm((mine // 128, n_y, width // n_y, 128), f32),
            vm((feat, crops), f32),
            vm((feat, crops), f32),
            dma((2,)), dma((2, 4)), dma((2,)), dma((2,)), dma((3,)), dma((3,)), dma((4,)), dma((4,)),
            dma((2,)), dma((2,)), dma((2,)), dma((2,)),
            dma((3,)), dma((mine // 128,)), dma((mine // 128,)), dma((2, 4)), dma((2, 4)),
            dma((2, 3)), dma((2, 3)), dma((1,)), dma((1,)), dma((2,)),
        ],
        compiler_params=pltpu.CompilerParams(
            collective_id=0, has_side_effects=True, vmem_limit_bytes=60 * 2**20
        ),
    )(t, s, w)
    return gf, gp, loss.reshape(())


def solution(mesh):
    placed = (P("proto", "crop"), P("proto", "crop"), P(None, "proto"))
    n_y = mesh.shape["crop"]
    n_chip = mesh.shape["proto"] // 2
    return jax.shard_map(
        functools.partial(on_device, n_y, n_chip),
        mesh=mesh,
        in_specs=placed,
        out_specs=(P("proto", "crop"), P("crop", "proto"), P()),
        check_vma=False,
    )
```

```python
import functools
import math

import jax
import jax.numpy as jnp
from jax import lax
from jax.experimental import pallas as pl
from jax.experimental.pallas import tpu as pltpu
from jax.sharding import PartitionSpec as P

MESH = pl.DeviceIdType.MESH
TEACHER_TEMP = 0.07
STUDENT_TEMP = 0.1
EPS = 1e-06
ITERS = 3
f32 = jnp.float32
bf16 = jnp.bfloat16
LANES = 128


def split(x):
    hi = x.astype(bf16)
    return hi, (x - hi.astype(f32)).astype(bf16)


def await_bytes(ref, sem):
    pltpu.make_async_copy(ref, ref, sem).wait()


def nn(a, b):
    return lax.dot_general(a, b, (((1,), (0,)), ((), ())), preferred_element_type=f32)


def nt(a, b):
    return lax.dot_general(a, b, (((1,), (1,)), ((), ())), preferred_element_type=f32)


def kernel(
    n_y, n_chip, scale, crops_all,
    t_ref, s_ref, w_ref,
    gf_ref, gp_ref, loss_ref,
    gt, gs, flat, zt_cat, zs_cat, z_cat, w_cat, e_ref, s_log, es_ref, g_hi, g_lo,
    er, esr, g_cat, far, vfar, tfar, a1, a2,
    tcol, vcol, col_out, col_in, ubuf, row_out, row_in, rs_flat, rs_src, rs_pair, rs_in,
    loss_in, loss_sum, part, final, t_raw, s_raw,
    sem_g_s, sem_g_r, sem_d_s, sem_d_r, sem_c_s, sem_c_r, sem_r_s, sem_r_r, sem_f_s, sem_f_r,
    sem_l_s, sem_l_r, sem_w, sem_y_s, sem_y_r, sem_a_s, sem_a_r,
    sem_e_s, sem_e_r, sem_v_s, sem_v_r, sem_x_s,
):
    p = lax.axis_index("proto")
    y = lax.axis_index("crop")
    chip = p // 2
    core = p % 2
    width, protos = w_ref.shape
    w_raw = s_log.at[0:width]
    t_copy = pltpu.make_async_copy(t_ref, t_raw, sem_w.at[1])
    s_copy = pltpu.make_async_copy(s_ref, s_raw, sem_w.at[2])
    w_copy = pltpu.make_async_copy(w_ref, w_raw, sem_w.at[0])
    t_copy.start()
    s_copy.start()
    w_copy.start()
    crops = e_ref.shape[0]
    n_ct = crops // LANES
    n_pt = protos // LANES
    feat = width // (2 * n_chip)
    n_plane = 2 * n_chip
    n_z = 8
    n_x = n_chip // n_z
    chip_x = chip // n_z
    chip_z = chip % n_z
    groups = (0, 2, 1, 3)
    ahead = lax.rem(y + 1, n_y)
    across = lax.rem(y + 2, n_y)
    behind = lax.rem(y + n_y - 1, n_y)
    mine = protos // n_y
    sibling = p + 1 - 2 * core

    bar = pltpu.get_barrier_semaphore()

    def plane_peers(go):
        def four(base):
            def step(i, c):
                for j in range(4):
                    go(lax.rem(p + base + 4 * i + j, n_plane))
                return c

            return step

        lax.fori_loop(0, (n_plane - 24) // 4, four(24), 0)
        lax.fori_loop(0, 5, four(1), 0)
        for k in range(21, 24):
            go(lax.rem(p + k, n_plane))

    def greet(other):
        pl.semaphore_signal(bar, inc=1, device_id=(other, y), device_id_type=MESH)

    plane_peers(greet)
    for i in range(1, n_y):
        for to in (p, sibling):
            pl.semaphore_signal(bar, inc=1, device_id=(to, lax.rem(y + i, n_y)), device_id_type=MESH)

    t_copy.wait()
    s_copy.wait()
    for src, dst in ((t_raw, gt), (s_raw, gs)):
        for j in range(feat):
            for ct in range(n_ct):
                k = n_ct * j + ct
                dst[0, chip, core, k : k + 1, :] = src[j : j + 1, ct * LANES : (ct + 1) * LANES]

    def prep_w(i, c):
        cols = pl.ds(pl.multiple_of(i * 256, 256), 256)
        w = w_raw[:, cols]
        w = w * (1.0 / jnp.sqrt(jnp.sum(w * w, axis=0, keepdims=True) + EPS))
        hi, lo = split(w)
        w_cat[0:width, cols] = hi
        w_cat[width : 2 * width, cols] = hi
        w_cat[2 * width : 3 * width, cols] = lo
        return c

    pl.semaphore_wait(bar, n_plane - 1 + 2 * (n_y - 1))

    def remote(src, dst, s, r, plane, crop):
        copy = pltpu.make_async_remote_copy(
            src_ref=src, dst_ref=dst, send_sem=s, recv_sem=r, device_id=(plane, crop), device_id_type=MESH
        )
        copy.start()
        return copy

    def gather_start(buf, k):
        for dx in groups[:2]:
            def go(dz, c):
                other = lax.rem(chip_x + dx, n_x) * n_z + lax.rem(chip_z + dz, n_z)
                here = buf.at[0, chip, core]
                remote(here, here, sem_g_s.at[k], sem_g_r.at[k, dx], other * 2 + core, y)
                return c

            lax.fori_loop(1 if dx == 0 else 0, n_z, go, 0)

    def slots_of(dx):
        return pl.ds(pl.multiple_of(lax.rem(chip_x + n_x - dx, n_x) * n_z, n_z), n_z)

    def gather_group(buf, k, dx):
        got = buf.at[0, pl.ds(0, n_z - 1 if dx == 0 else n_z), core]
        await_bytes(got, sem_g_r.at[k, dx])
        block = buf.at[0, slots_of(dx), core]
        if dx == 0:
            for far_x in (1, 3):
                over = lax.rem(chip_x + far_x, n_x) * n_z + chip_z
                remote(block, block, sem_x_s.at[k], sem_g_r.at[k, far_x], over * 2 + core, y)
        remote(block, block, sem_d_s.at[k], sem_d_r.at[k], sibling, y)

    def spread_group(buf, k, dx):
        block = buf.at[0, slots_of(dx), core]
        remote(block, buf.at[n_y - 1, slots_of(dx), core], sem_a_s.at[k, 0], sem_a_r.at[k, 0], p, ahead)
        remote(block, buf.at[1, slots_of(dx), core], sem_a_s.at[k, 1], sem_a_r.at[k, 1], p, behind)

    def gather_finish(buf, k):
        await_bytes(buf.at[0, :, core], sem_d_r.at[k])

    def share(buf, k, rel):
        block = buf.at[rel, :, core]
        remote(block, block, sem_e_s.at[k, rel - 1], sem_e_r.at[k, rel - 1], sibling, y)

    def near_finish(buf, k):
        await_bytes(buf.at[n_y - 1, :, core], sem_a_r.at[k, 0])
        await_bytes(buf.at[1, :, core], sem_a_r.at[k, 1])
        share(buf, k, 1)
        share(buf, k, 3)

    def relay(buf, k):
        low, high = pl.ds(0, n_chip // 2), pl.ds(n_chip // 2, n_chip // 2)
        remote(buf.at[3, low, core], buf.at[2, low, core], sem_a_s.at[k, 2], sem_a_r.at[k, 2], p, ahead)
        remote(buf.at[1, high, core], buf.at[2, high, core], sem_a_s.at[k, 3], sem_a_r.at[k, 3], p, behind)

    def far_finish(buf, k):
        for i in (2, 3):
            await_bytes(buf.at[2, pl.ds(0, n_chip // 2), core], sem_a_r.at[k, i])
        share(buf, k, 2)

    def unit(buf, rel, temp, cat, keep):
        flat[...] = buf[rel].reshape(flat.shape)
        for ct in range(n_ct):
            rows = pl.ds(ct * LANES, LANES)
            x = flat[pl.ds(ct, width, stride=n_ct), :]
            x = x * (1.0 / jnp.sqrt(jnp.sum(x * x, axis=0, keepdims=True) + EPS))
            if keep:
                hi, lo = split(x)
                base = rel * 3 * crops + ct * LANES
                z_cat[:, base : base + LANES] = hi
                z_cat[:, crops + base : crops + base + LANES] = lo
                z_cat[:, 2 * crops + base : 2 * crops + base + LANES] = hi
            xt = (x * (1.0 / temp)).T
            hi, lo = split(xt)
            cat[rows, 0:width] = hi
            cat[rows, width : 2 * width] = lo
            cat[rows, 2 * width : 3 * width] = hi

    def other_block(buf, k, rel, temp, dst, keep):
        await_bytes(buf.at[rel, :, core], sem_e_r.at[k, rel - 1])
        unit(buf, rel, temp, zt_cat, keep)
        cols = pl.ds(pl.multiple_of(y * mine, mine), mine)
        dst[rel - 1] = jnp.exp(nn(zt_cat[...], w_cat[:, cols]))

    def col_start(k):
        col_in[k, pl.ds(y, 1)] = col_out[k : k + 1]
        for i in range(1, n_y):
            pltpu.make_async_remote_copy(
                src_ref=col_out.at[k],
                dst_ref=col_in.at[k, y],
                send_sem=sem_c_s.at[k],
                recv_sem=sem_c_r.at[k],
                device_id=(p, lax.rem(y + i, n_y)),
                device_id_type=MESH,
            ).start()

    def col_finish(k):
        await_bytes(col_in.at[k, pl.ds(0, n_y - 1)], sem_c_r.at[k])
        total = col_in[k, 0]
        for i in range(1, n_y):
            total = total + col_in[k, i]
        ubuf[...] = 1.0 / total

    def row_start(k):
        row_in[k, pl.ds(p, 1)] = row_out[k : k + 1]

        def go(other):
            remote(row_out.at[k], row_in.at[k, p], sem_r_s.at[k], sem_r_r.at[k], other, y)

        plane_peers(go)

    def row_finish(k):
        await_bytes(row_in.at[k, pl.ds(0, n_plane - 1)], sem_r_r.at[k])
        return jnp.sum(row_in[k], axis=0)

    def to_rows(k):
        for ct in range(n_ct):
            block = tcol[ct * LANES : (ct + 1) * LANES, :].T
            row_out[k, ct : ct + 1, :] = jnp.sum(block, axis=0, keepdims=True)

    def to_column(values):
        for ct in range(n_ct):
            row = jnp.broadcast_to(values[ct : ct + 1, :], (LANES, LANES))
            vcol[ct * LANES : (ct + 1) * LANES, :] = row.T

    chunk = 64

    def lane_fold(x):
        total = x[:, 0:LANES]
        for j in range(1, n_pt):
            total = total + x[:, j * LANES : (j + 1) * LANES]
        return total

    def scaled_fold(rows):
        total = None
        for j in range(n_pt):
            x = e_ref[rows, j * LANES : (j + 1) * LANES]
            x = x * ubuf[j : j + 1, :]
            total = x if total is None else total + x
        return total

    def row_pass(k):
        def go(i, c):
            rows = pl.ds(pl.multiple_of(i * chunk, chunk), chunk)
            tcol[rows, :] = scaled_fold(rows)
            return c

        lax.fori_loop(0, crops // chunk, go, 0)
        to_rows(k)

    def col_pass(k):
        def go(i, acc):
            rows = pl.ds(pl.multiple_of(i * 32, 32), 32)
            v = vcol[rows, :]
            out = []
            for j in range(n_pt):
                x = e_ref[rows, j * LANES : (j + 1) * LANES] * v
                out.append(acc[j] + jnp.sum(x.reshape(4, 8, LANES), axis=0))
            return tuple(out)

        acc = lax.fori_loop(0, crops // 32, go, tuple(jnp.zeros((8, LANES), f32) for _ in range(n_pt)))
        for j in range(n_pt):
            col_out[k, j : j + 1, :] = jnp.sum(acc[j], axis=0, keepdims=True)

    gather_start(gt, 0)
    w_copy.wait()
    lax.fori_loop(0, protos // 256, prep_w, 0)
    for dx in groups:
        gather_group(gt, 0, dx)
        spread_group(gt, 0, dx)
    gather_start(gs, 1)
    gather_finish(gt, 0)
    unit(gt, 0, TEACHER_TEMP, zt_cat, False)

    wide = 1024

    def teacher_block(i, c):
        cols = pl.ds(pl.multiple_of(i * wide, wide), wide)
        e = jnp.exp(nn(zt_cat[...], w_cat[:, cols]))
        e_ref[:, cols] = e
        sums = jnp.sum(e, axis=0, keepdims=True)
        for j in range(wide // LANES):
            col_out[0, pl.ds(wide // LANES * i + j, 1), :] = sums[:, j * LANES : (j + 1) * LANES]
        return c

    lax.fori_loop(0, protos // wide, teacher_block, 0)
    col_start(0)
    gather_group(gs, 1, 0)
    near_finish(gt, 0)
    col_finish(0)
    row_pass(0)
    row_start(0)
    spread_group(gs, 1, 0)
    for dx in groups[1:]:
        gather_group(gs, 1, dx)
        if dx != groups[3]:
            spread_group(gs, 1, dx)
    gather_finish(gs, 1)
    unit(gs, 0, STUDENT_TEMP, zs_cat, True)

    def student_block(i, c):
        cols = pl.ds(pl.multiple_of(i * wide, wide), wide)
        s = nn(zs_cat[...], w_cat[:, cols])
        s_log[:, cols] = s
        es_ref[:, cols] = jnp.exp(s)
        return c

    lax.fori_loop(0, protos // wide, student_block, 0)
    def features_of(dst, scale_u):
        def go(r, c):
            rows = pl.ds(pl.multiple_of(r * 64, 64), 64)
            cross = None
            for j in range(n_pt):
                lanes = slice(j * LANES, (j + 1) * LANES)
                if scale_u:
                    g = e_ref[rows, lanes] * ubuf[j : j + 1, :]
                    term = g * s_log[rows, lanes]
                    cross = term if cross is None else cross + term
                else:
                    g = es_ref[rows, lanes]
                hi, lo = split(g)
                g_hi[rows, lanes] = hi
                g_lo[rows, lanes] = lo
            if scale_u:
                tcol[rows, :] = cross
            return c

        lax.fori_loop(0, crops // 64, go, 0)
        w_hi, w_lo = w_cat[0:width, :], w_cat[2 * width : 3 * width, :]
        dst[...] = nt(w_hi, g_hi[...]) + nt(w_hi, g_lo[...]) + nt(w_lo, g_hi[...])

    for k in (1, 2):
        to_column(1.0 / row_finish(k - 1))
        col_pass(k)
        col_start(k)
        if k == 1:
            relay(gt, 0)

            def fold(i, c):
                rows = pl.ds(pl.multiple_of(i * chunk, chunk), chunk)
                tcol[rows, :] = lane_fold(es_ref[rows, :])
                return c

            lax.fori_loop(0, crops // chunk, fold, 0)
            to_rows(3)
            row_start(3)
            other_block(gt, 0, 1, TEACHER_TEMP, er, False)
        else:
            relay(gs, 1)
            other_block(gt, 0, 2, TEACHER_TEMP, er, False)
            other_block(gs, 1, 1, STUDENT_TEMP, esr, True)
        col_finish(k)
        row_pass(k)
        row_start(k)
        if k == 1:
            spread_group(gs, 1, groups[3])
            other_block(gt, 0, 3, TEACHER_TEMP, er, False)
            features_of(a1, False)
            far_finish(gt, 0)
            near_finish(gs, 1)
    features_of(a2, True)
    far_finish(gs, 1)
    other_block(gs, 1, 3, STUDENT_TEMP, esr, True)
    other_block(gs, 1, 2, STUDENT_TEMP, esr, True)
    last = row_finish(2)
    student_total = row_finish(3)
    far[0, 0:n_ct, :] = scale / last
    far[0, n_ct : 2 * n_ct, :] = scale / student_total
    for i in range(1, n_y):
        remote(far.at[0], far.at[n_y - i], sem_v_s.at[0], sem_v_r.at[0], p, lax.rem(y + i, n_y))

    def spread_columns(rel, v_dst, t_dst):
        for ct in range(n_ct):
            rows = slice(ct * LANES, (ct + 1) * LANES)
            for dst, k in ((v_dst, ct), (t_dst, n_ct + ct)):
                row = jnp.broadcast_to(far[rel, k : k + 1, :], (LANES, LANES))
                dst[rows, :] = row.T

    out_rows = width // n_y
    half = LANES

    def rows_of(d):
        return pl.ds(pl.multiple_of(d * out_rows, 8), out_rows)

    def grads_of(rel, c0):
        lanes = pl.ds(pl.multiple_of(c0 * LANES, LANES), LANES)
        here = pl.ds(pl.multiple_of(y * mine + c0 * LANES, LANES), LANES)
        u = ubuf[pl.ds(y * (mine // LANES) + c0, 1), :]

        def go(r, c):
            rows = pl.ds(pl.multiple_of(r * 64, 64), 64)
            v = vfar[rel, rows, :]
            t = tfar[rel, rows, :]
            if rel == 0:
                e, es = e_ref[rows, here], es_ref[rows, here]
            else:
                e, es = er[rel - 1, rows, lanes], esr[rel - 1, rows, lanes]
            hi, lo = split(es * t - e * u * v)
            base = pl.multiple_of(rel * 3 * crops + r * 64, 64)
            g_cat[pl.ds(base, 64), lanes] = hi
            g_cat[pl.ds(base + crops, 64), lanes] = hi
            g_cat[pl.ds(base + 2 * crops, 64), lanes] = lo
            return c

        lax.fori_loop(0, crops // 64, go, 0)

    def proto_part(h, carry):
        for rel in range(1, n_y):
            grads_of(rel, h)
        lanes = pl.ds(pl.multiple_of(h * half, half), half)
        part[h] = nn(z_cat[...], g_cat[:, lanes])
        final[h, pl.ds(y, 1)] = part[h, rows_of(y)][None]
        for i in (2, 1, 3):
            to = lax.rem(y + i, n_y)
            remote(part.at[h, rows_of(to)], final.at[h, y], sem_y_s.at[h], sem_y_r.at[h], p, to)
        return carry

    spread_columns(0, vfar.at[0], tfar.at[0])

    cross = jnp.sum(tcol[...] * vfar[0], axis=0, keepdims=True)
    lse = jnp.sum(jnp.log(student_total), axis=0, keepdims=True)
    loss_in[pl.ds(2 * y + core, 1)] = (lse * (1.0 / n_plane) - cross * (1.0 / scale))[None]
    for i in range(n_y):
        for c in range(2):
            if i or c:
                here = loss_in.at[2 * y + core]
                to = 2 * chip + lax.rem(core + c, 2)
                remote(here, here, sem_l_s.at[0], sem_l_r.at[0], to, lax.rem(y + i, n_y))
    for ct in range(n_ct):
        lanes = slice(ct * LANES, (ct + 1) * LANES)
        t, v = far[0, n_ct + ct : n_ct + ct + 1, :], far[0, ct : ct + 1, :]
        rs_flat[pl.ds(ct, width, stride=n_ct), :] = a1[:, lanes] * t - a2[:, lanes] * v
    rs_src[...] = rs_flat[...].reshape(rs_src.shape)
    pair = pltpu.make_async_remote_copy(
        src_ref=rs_src.at[:, 1 - core],
        dst_ref=rs_pair,
        send_sem=sem_f_s.at[0],
        recv_sem=sem_f_r.at[0],
        device_id=(p + 1 - 2 * core, y),
        device_id_type=MESH,
    )
    pair.start()
    lax.fori_loop(0, mine // half, lambda h, c: (grads_of(0, h), c)[1], 0)
    pair.wait()
    rs_pair[...] += rs_src[:, core]
    rs_in[pl.ds(chip, 1)] = rs_pair[pl.ds(chip, 1)]

    def scatter(i, c):
        other = lax.rem(chip + i, n_chip)
        pltpu.make_async_remote_copy(
            src_ref=rs_pair.at[other],
            dst_ref=rs_in.at[chip],
            send_sem=sem_f_s.at[1],
            recv_sem=sem_f_r.at[1],
            device_id=(other * 2 + core, y),
            device_id_type=MESH,
        ).start()
        return c

    lax.fori_loop(1, n_chip, scatter, 0)
    await_bytes(far.at[pl.ds(1, n_y - 1)], sem_v_r.at[0])
    for rel in range(1, n_y):
        spread_columns(rel, vfar.at[rel], tfar.at[rel])
    lax.fori_loop(0, mine // half, proto_part, 0)
    await_bytes(loss_in.at[pl.ds(0, 2 * n_y - 1)], sem_l_r.at[0])
    loss_sum[pl.ds(chip, 1)] = jnp.sum(loss_in[...], axis=0, keepdims=True)

    def scatter_loss(i, c):
        here = loss_sum.at[chip]
        remote(here, here, sem_l_s.at[1], sem_l_r.at[1], lax.rem(chip + i, n_chip) * 2 + core, y)
        return c

    lax.fori_loop(1, n_chip, scatter_loss, 0)

    await_bytes(rs_in.at[pl.ds(0, n_chip - 1)], sem_f_r.at[1])
    total = jnp.sum(rs_in[...], axis=0)
    for j in range(feat):
        for ct in range(n_ct):
            k = n_ct * j + ct
            gf_ref[j : j + 1, ct * LANES : (ct + 1) * LANES] = total[k : k + 1, :]
    for h in range(mine // half):
        await_bytes(final.at[h, pl.ds(0, n_y - 1)], sem_y_r.at[h])
        for q in range(n_y):
            gp_ref[:, q * mine + h * half : q * mine + (h + 1) * half] = final[h, q]
    await_bytes(loss_sum.at[pl.ds(0, n_chip - 1)], sem_l_r.at[1])
    loss_ref[0, 0] = jnp.sum(jnp.sum(loss_sum[...], axis=0)) * (1.0 / crops_all)

    for k, buf in ((0, gt), (1, gs)):
        await_bytes(buf.at[0, pl.ds(0, 2 * n_z - 1), core], sem_g_s.at[k])
        await_bytes(buf.at[0, pl.ds(0, 2 * n_z), core], sem_x_s.at[k])
        await_bytes(buf.at[0, :, core], sem_d_s.at[k])
        for i in range(2):
            await_bytes(buf.at[0, :, core], sem_a_s.at[k, i])
            await_bytes(buf.at[0, pl.ds(0, n_chip // 2), core], sem_a_s.at[k, 2 + i])
        for i in range(n_y - 1):
            await_bytes(buf.at[0, :, core], sem_e_s.at[k, i])
    await_bytes(far.at[pl.ds(1, n_y - 1)], sem_v_s.at[0])
    for h in range(mine // half):
        await_bytes(final.at[h, pl.ds(0, n_y - 1)], sem_y_s.at[h])
    await_bytes(loss_in.at[pl.ds(0, 2 * n_y - 1)], sem_l_s.at[0])
    await_bytes(loss_sum.at[pl.ds(0, n_chip - 1)], sem_l_s.at[1])
    await_bytes(rs_in.at[pl.ds(0, n_chip - 1)], sem_f_s.at[1])
    for k in range(3):
        await_bytes(col_in.at[k, pl.ds(0, n_y - 1)], sem_c_s.at[k])
    for k in range(4):
        await_bytes(row_in.at[k, pl.ds(0, n_plane - 1)], sem_r_s.at[k])


def on_device(n_y, n_chip, t, s, w):
    width, protos = w.shape
    feat, crops = t.shape
    n_ct = crops // LANES
    n_pt = protos // LANES
    n_plane = 2 * n_chip
    scale = math.sqrt(protos * n_plane) / STUDENT_TEMP
    vm = pltpu.VMEM
    dma = pltpu.SemaphoreType.DMA
    slots = (n_chip, 2, feat * n_ct, LANES)
    mine = protos // n_y
    gf, gp, loss = pl.pallas_call(
        functools.partial(kernel, n_y, n_chip, scale, crops * n_y),
        out_shape=(
            pltpu.VMEM((feat, crops), f32),
            pltpu.VMEM((width // n_y, protos), f32),
            jax.ShapeDtypeStruct((1, 1), f32),
        ),
        in_specs=[
            pl.BlockSpec(memory_space=pl.ANY),
            pl.BlockSpec(memory_space=pl.ANY),
            pl.BlockSpec(memory_space=pl.ANY),
        ],
        out_specs=(
            pl.BlockSpec(memory_space=vm),
            pl.BlockSpec(memory_space=vm),
            pl.BlockSpec(memory_space=pltpu.SMEM),
        ),
        scratch_shapes=[
            vm((n_y,) + slots, f32),
            vm((n_y,) + slots, f32),
            vm((width * n_ct, LANES), f32),
            vm((crops, 3 * width), bf16),
            vm((crops, 3 * width), bf16),
            vm((width, 3 * n_y * crops), bf16),
            vm((3 * width, protos), bf16),
            vm((crops, protos), f32),
            vm((crops, protos), f32),
            vm((crops, protos), f32),
            vm((crops, protos), bf16),
            vm((crops, protos), bf16),
            vm((n_y - 1, crops, mine), f32),
            vm((n_y - 1, crops, mine), f32),
            vm((3 * n_y * crops, mine), bf16),
            vm((n_y, 2 * n_ct, LANES), f32),
            vm((n_y, crops, LANES), f32),
            vm((n_y, crops, LANES), f32),
            vm((width, crops), f32),
            vm((width, crops), f32),
            vm((crops, LANES), f32),
            vm((crops, LANES), f32),
            vm((3, n_pt, LANES), f32),
            vm((3, n_y, n_pt, LANES), f32),
            vm((n_pt, LANES), f32),
            vm((4, n_ct, LANES), f32),
            vm((4, n_plane, n_ct, LANES), f32),
            vm((width * n_ct, LANES), f32),
            vm(slots, f32),
            vm(slots[:1] + slots[2:], f32),
            vm(slots[:1] + slots[2:], f32),
            vm((2 * n_y, 1, LANES), f32),
            vm((n_chip, 1, LANES), f32),
            vm((mine // 128, width, 128), f32),
            vm((mine // 128, n_y, width // n_y, 128), f32),
            vm((feat, crops), f32),
            vm((feat, crops), f32),
            dma((2,)), dma((2, 4)), dma((2,)), dma((2,)), dma((3,)), dma((3,)), dma((4,)), dma((4,)),
            dma((2,)), dma((2,)), dma((2,)), dma((2,)),
            dma((3,)), dma((mine // 128,)), dma((mine // 128,)), dma((2, 4)), dma((2, 4)),
            dma((2, 3)), dma((2, 3)), dma((1,)), dma((1,)), dma((2,)),
        ],
        compiler_params=pltpu.CompilerParams(
            collective_id=0, has_side_effects=True, vmem_limit_bytes=60 * 2**20
        ),
    )(t, s, w)
    return gf, gp, loss.reshape(())


def solution(mesh):
    placed = (P("proto", "crop"), P("proto", "crop"), P(None, "proto"))
    n_y = mesh.shape["crop"]
    n_chip = mesh.shape["proto"] // 2
    return jax.shard_map(
        functools.partial(on_device, n_y, n_chip),
        mesh=mesh,
        in_specs=placed,
        out_specs=(P("proto", "crop"), P("crop", "proto"), P()),
        check_vma=False,
    )
```
